512 devices in a mesh: dp: 64 (over y, x, z_hi), fsdp: 8 (over z_lo, core).
Axes of the slice: x: 4, y: 8, z: 8 (z_hi: 2, z_lo: 4; z = z_hi * 4 + z_lo), core: 2. Of those that a mesh axis runs over, the one named last changes fastest.
Arguments:
- tokens: bfloat16 [24576, 4096], P('dp'), may hold values from -6 to 6
- grad_out: bfloat16 [24576, 11008], P('dp', 'fsdp'), may hold values from -0.375 to 0.375
- subspace_basis: bfloat16 [4096, 512], P('dp'), may hold values from -0.09375 to 0.09375
- first_moment: float32 [512, 11008], P('dp', 'fsdp'), may hold values from -18 to 18
- second_moment: float32 [512, 11008], P('dp', 'fsdp'), may hold values from 0.03 to 0.3
Outputs:
- new_first: float32 [512, 11008], P('dp', 'fsdp')
- new_second: float32 [512, 11008], P('dp', 'fsdp')
- weight_update: bfloat16 [4096, 11008], P('dp')
The draws below stay inside these ranges and needn't reach their ends.
All inputs are finite; a program needn't handle non-finite values.
Results may differ from the reference program's by a relative error of at most 0.0052.
Values may be sent and summed in bfloat16 or wider, within the bound.
A program may use at most 64 MiB of HBM per device.

```python
import math
import jax
import jax.numpy as jnp

D = 4096
FF = 11008
RANK = 512
TOKENS = 24576


def levels(own_key, extent, cuts, low, high):
    gain, own = 1.0, jax.random.fold_in(own_key, 6)
    for position, shards_of in cuts:
        steps = jnp.exp(jax.random.uniform(jax.random.fold_in(own, position), (shards_of,), jnp.float32, low / len(cuts), high / len(cuts)))
        gain = gain * jnp.repeat(steps, extent[position] // shards_of).reshape([-1 if axis == position else 1 for axis in range(len(extent))])
    return gain


def noise(key, extent, width, bound, shards=(), dtype=jnp.bfloat16):
    result = jax.random.normal(key, extent, jnp.float32) * width
    if len(shards) > 0:
        result = levels(key, extent, shards, -0.22, 0.18) * result
    return jnp.clip(result, min=-bound, max=bound).astype(dtype)


def setup_inputs(seed: int = 0) -> dict:
    arg_keys = jax.random.split(jax.random.key(seed), 6)
    tokens = noise(arg_keys[0], (TOKENS, D), 1.0, 6.0, ((0, 64),))
    grad_out = noise(arg_keys[1], (TOKENS, FF), (TOKENS // 100) ** -0.5, 0.375, ((0, 64), (1, 8)))
    subspace_basis = noise(arg_keys[2], (D, RANK), D ** -0.5, 0.09375, ((0, 64),))
    first_moment = noise(arg_keys[3], (RANK, FF), 3.0, 18.0, ((0, 64), (1, 8)), jnp.float32)
    second_moment = jnp.clip(jnp.exp(math.log(0.3) - 2.3025852 * jax.random.uniform(arg_keys[4], (RANK, FF), jnp.float32) ** levels(arg_keys[4], (RANK, FF), ((0, 64), (1, 8)), -0.2, 0.2)), 0.03, 0.3)
    return dict(tokens=tokens, grad_out=grad_out, subspace_basis=subspace_basis, first_moment=first_moment, second_moment=second_moment)


beta_one = 0.9
beta_two = 0.999
correct_one = 1.0 - 0.9 ** 10
correct_two = 1.0 - 0.999 ** 10

def reference(tokens, grad_out, subspace_basis, first_moment, second_moment):
    projected = jnp.dot(tokens, subspace_basis, preferred_element_type=jnp.float32).astype(jnp.bfloat16)
    low_grad = jnp.dot(projected.T, grad_out, preferred_element_type=jnp.float32)
    new_first = beta_one * first_moment + (1.0 - beta_one) * low_grad
    new_second = beta_two * second_moment + (1.0 - beta_two) * low_grad * low_grad
    direction = (new_first / correct_one / (jnp.sqrt(new_second / correct_two) + 1e-08)).astype(jnp.bfloat16)
    weight_update = jnp.dot(subspace_basis, direction, preferred_element_type=jnp.float32).astype(jnp.bfloat16)
    return (new_first, new_second, weight_update)
```

```python
import functools

import jax
import jax.numpy as jnp
from jax import lax
from jax.experimental import pallas as pl
from jax.experimental.pallas import tpu as pltpu
from jax.sharding import PartitionSpec as P

beta_one = 0.9
beta_two = 0.999
correct_one = 1.0 - 0.9**10
correct_two = 1.0 - 0.999**10

X = 4
Z_HI, Z_LO, CORES = 2, 4, 2
RING = Z_HI * Z_LO
PART_A = 640
COPIES = 160

MESH = pl.DeviceIdType.MESH
F32, BF16 = jnp.float32, jnp.bfloat16


def wrap(value, n):
    return lax.rem(value + n, n)


def interleave(*steps):
    steps = list(steps)
    while steps:
        steps = [step for step in steps if next(step, "end") != "end"]


def kernel(
    Y, tokens, grad, basis, first, second,
    new_first, new_second, update,
    tok_v, grad_v, basis_v, bas, proj, first_v, second_v, nf_v, ns_v,
    own_a, own_b, mid_a, mid_b, sum_a, sum_b,
    sa1, ra1, sa2, ra2, sb1, rb1, sb2, rb2, pair_sa, pair_ra, pair_sb, pair_rb,
    dir_a, dir_b, send_a, send_b, upd_a, upd_b,
    send_sem, recv_sem, load_sem,
):
    dp, fs = lax.axis_index("dp"), lax.axis_index("fsdp")
    zh, xy = lax.rem(dp, Z_HI), dp // Z_HI
    x, y = lax.rem(xy, X), xy // X
    core, zl = lax.rem(fs, CORES), fs // CORES
    z = zh * Z_LO + zl
    half_tokens = tok_v.shape[0]
    depth = bas.shape[4]
    rows = basis_v.shape[1]
    cols = grad.shape[1]
    parts = ((0, PART_A), (PART_A, cols - PART_A))

    def device(y_, x_, z_, core_):
        return ((y_ * X + x_) * Z_HI + z_ // Z_LO, lax.rem(z_, Z_LO) * CORES + core_)

    at_y = lambda t: device(t, x, z, core)
    at_x = lambda t: device(y, t, z, core)
    at_z = lambda t: device(y, x, t, core)
    sibling = device(y, x, z, 1 - core)
    partner = at_z(wrap(z + Z_LO, RING))

    sent = []

    def send(src, dst, target):
        k = len(sent)
        copy = pltpu.make_async_remote_copy(
            src_ref=src, dst_ref=dst, send_sem=send_sem.at[k], recv_sem=recv_sem.at[k],
            device_id=target, device_id_type=MESH,
        )
        copy.start()
        sent.append(copy)
        return copy

    def ring_gather(n, pos, target, block, half=None, arrived=None):
        flying = {}
        for s in range(n // 2):
            for d, h in ((1, 0), (-1, 1)):
                t = wrap(pos - d * s, n)
                if s:
                    flying[d].wait_recv()
                    if arrived:
                        arrived(t)
                if s < n // 2 - 1:
                    ref = block(t)
                elif half:
                    ref = half(t, h)
                elif d == 1:
                    ref = block(t)
                else:
                    flying.pop(d, None)
                    continue
                flying[d] = send(ref, ref, target(wrap(pos + d, n)))
            yield
        for copy in flying.values():
            copy.wait_recv()
        if arrived:
            arrived(wrap(pos + n // 2, n))

    def ring_scatter(n, pos, target, own, sbuf, rbuf, result, split):
        flying, last = {}, {}
        size = own.shape[1]
        for s in range(n // 2):
            for i, d in ((0, 1), (1, -1)):
                t = wrap(pos + d * (n // 2 - s), n)
                whole = pl.ds(0, size)
                part = pl.ds(i * (size // 2), size // 2) if split else whole
                if s == 0:
                    if not split and i == 1:
                        continue
                    sbuf[i, 0, part] = own[t, part].astype(BF16)
                    flying[i] = send(sbuf.at[i, 0, part], rbuf.at[i, 0, part], target(wrap(pos + d, n)))
                    last[i] = (0, part)
                    continue
                if i in flying:
                    flying[i].wait_recv()
                    before, taken = last[i]
                    sbuf[i, s, taken] = (own[t, taken] + rbuf[i, before, taken].astype(F32)).astype(BF16)
                    if split and s == 1:
                        other = pl.ds((1 - i) * (size // 2), size // 2)
                        sbuf[i, s, other] = own[t, other].astype(BF16)
                else:
                    sbuf[i, s] = own[t].astype(BF16)
                flying[i] = send(sbuf.at[i, s], rbuf.at[i, s], target(wrap(pos + d, n)))
                last[i] = (s, whole)
            yield
        total = own[pos]
        for i in flying:
            flying[i].wait_recv()
        if n == 2 and split:
            low = rbuf[0, 0, pl.ds(0, size // 2)].astype(F32)
            high = rbuf[1, 0, pl.ds(size // 2, size // 2)].astype(F32)
            total = total + jnp.concatenate([low, high], axis=0)
        else:
            for i in flying:
                total = total + rbuf[i, last[i][0]].astype(F32)
        result[...] = total.reshape(result.shape)

    loads = [
        pltpu.make_async_copy(basis, basis_v.at[zh], load_sem.at[0]),
        pltpu.make_async_copy(tokens.at[pl.ds(core * half_tokens, half_tokens)], tok_v, load_sem.at[1]),
        pltpu.make_async_copy(grad, grad_v, load_sem.at[2]),
        pltpu.make_async_copy(first, first_v.at[zh], load_sem.at[3]),
        pltpu.make_async_copy(second, second_v.at[zh], load_sem.at[4]),
    ]
    for load in loads:
        load.start()

    barrier = pltpu.get_barrier_semaphore()
    near = [at_z(wrap(z + k - RING, RING)) for k in range(1, RING)] + [sibling]
    for d in (1, -1):
        near += [at_y(wrap(y + d, Y)), at_x(wrap(x + d, X))]
    for target in near:
        pl.semaphore_signal(barrier, inc=1, device_id=target, device_id_type=MESH)
    pl.semaphore_wait(barrier, len(near))

    loads[0].wait()
    share = pl.ds(core * (rows // 2), rows // 2)
    lanes = pl.ds(zl * depth_of(bas), depth_of(bas))
    bas[y, x, zh, share] = basis_v[zh, share, lanes]
    pair = send(bas.at[y, x, zh, share], bas.at[y, x, zh, share], partner)
    loads[3].wait()
    loads[4].wait()
    basis_pair = send(basis_v.at[zh], basis_v.at[zh], partner)
    first_pair = send(first_v.at[zh], first_v.at[zh], partner)
    second_pair = send(second_v.at[zh], second_v.at[zh], partner)
    pair.wait_recv()
    interleave(
        ring_gather(
            X, x, at_x,
            lambda t: bas.at[y, t, :, share],
            lambda t, h: bas.at[y, t, pl.ds(h, 1), share],
        )
    )
    to_sibling = []

    def hand_over(t):
        ref = bas.at[t, :, :, share]
        to_sibling.append(send(ref, ref, sibling))

    hand_over(y)
    interleave(
        ring_gather(
            Y, y, at_y,
            lambda t: bas.at[t, :, :, share],
            lambda t, h: bas.at[t, pl.ds(h * (X // 2), X // 2), :, share],
            hand_over,
        )
    )
    for copy in to_sibling:
        copy.wait_recv()

    loads[1].wait()
    mine = pl.ds(core * half_tokens, half_tokens)
    proj[zl, mine] = jnp.dot(
        tok_v[...], bas[...].reshape(-1, depth_of(bas)), preferred_element_type=F32
    ).astype(BF16)
    ref = proj.at[zl, mine]
    beside = [send(ref, ref, sibling)]
    along = [send(ref, ref, at_z(zh * Z_LO + wrap(zl + k - Z_LO, Z_LO))) for k in range(1, Z_LO)]
    loads[2].wait()
    wide = own_a.shape[1] // 16 * 16
    per = depth_of(bas) // wide
    for k in range(Z_LO):
        r = wrap(zl - k, Z_LO)
        if k:
            along[k - 1].wait_recv()
            ref = proj.at[r, mine]
            beside.append(send(ref, ref, sibling))
        beside[k].wait_recv()
        part = lax.dot_general(
            proj[r], grad_v[...], (((0,), (0,)), ((), ())), preferred_element_type=F32
        )
        own_a[pl.ds(r * per, per)] = part[:, :PART_A].reshape(per, wide, PART_A)
        part_b = part[:, PART_A:].reshape(per, X, 16, cols - PART_A)
        for t in range(X):
            own_b[t, pl.ds(r * per, per)] = part_b[:, t]

    basis_pair.wait_recv()
    first_pair.wait_recv()
    second_pair.wait_recv()

    def column_part(number):
        low, width = parts[number]
        total, pair_s, pair_r = ((sum_a, pair_sa, pair_ra), (sum_b, pair_sb, pair_rb))[number]
        if number == 0:
            yield from ring_scatter(Y, y, at_y, own_a, sa1, ra1, mid_a, True)
            yield from ring_scatter(X, x, at_x, mid_a, sa2, ra2, total, False)
        else:
            yield from ring_scatter(X, x, at_x, own_b, sb1, rb1, mid_b, True)
            yield from ring_scatter(Y, y, at_y, mid_b, sb2, rb2, total, False)
        pair_s[...] = total[...].astype(BF16)
        copy = send(pair_s, pair_r, partner)
        yield
        copy.wait_recv()
        low_grad = total[...] + pair_r[...].astype(F32)
        span = pl.ds(low, width)
        old_first = first_v[:, :, span].reshape(low_grad.shape)
        old_second = second_v[:, :, span].reshape(low_grad.shape)
        fresh_first = beta_one * old_first + (1.0 - beta_one) * low_grad
        fresh_second = beta_two * old_second + (1.0 - beta_two) * low_grad * low_grad
        nf_v[:, :, span] = fresh_first.reshape(Z_HI, -1, width)
        ns_v[:, :, span] = fresh_second.reshape(Z_HI, -1, width)
        direction = (
            fresh_first / correct_one / (jnp.sqrt(fresh_second / correct_two) + 1e-08)
        ).astype(BF16)
        whole = (dir_a, dir_b)[number]
        whole[y, x] = direction
        if number == 0:
            yield from ring_gather(X, x, at_x, lambda t: whole.at[y, t])
            yield from ring_gather(
                Y, y, at_y, lambda t: whole.at[t],
                lambda t, h: whole.at[t, pl.ds(h * (X // 2), X // 2)],
            )
        else:
            yield from ring_gather(Y, y, at_y, lambda t: whole.at[t, x])
            yield from ring_gather(
                X, x, at_x, lambda t: whole.at[:, t],
                lambda t, h: whole.at[pl.ds(h * (Y // 2), Y // 2), t],
            )
        out_s, out_r = ((send_a, upd_a), (send_b, upd_b))[number]
        block = jnp.dot(
            basis_v[...].reshape(Z_HI * rows, -1), whole[...].reshape(-1, width),
            preferred_element_type=F32,
        ).astype(BF16)
        out_s[...] = block.reshape(out_s.shape)
        moving = {}
        for step in (1, -1):
            to = wrap(z + step, RING)
            moving[step] = send(out_s.at[to // Z_LO], out_r.at[zl, core], at_z(to))
        for step in (2, -2):
            to = wrap(z + step, RING)
            cut = pl.ds(0 if step > 0 else rows // 2, rows // 2)
            moving[step] = send(out_s.at[to // Z_LO, cut], out_r.at[zl, core, cut], at_z(to))
        out_r[zl, core] = out_s[zh]
        across = [send(out_r.at[zl, core], out_r.at[zl, core], sibling)]
        yield
        for step in (1, -1):
            moving[step].wait_recv()
            ref = out_r.at[wrap(zl - step, Z_LO), core]
            across.append(send(ref, ref, sibling))
        yield
        moving[2].wait_recv()
        moving[-2].wait_recv()
        ref = out_r.at[wrap(zl + 2, Z_LO), core]
        across.append(send(ref, ref, sibling))
        yield
        for copy in across:
            copy.wait_recv()
        for block in range(Z_LO):
            for c in range(CORES):
                at = (block * CORES + c) * cols + low
                update[:, at : at + width] = out_r[block, c]

    interleave(column_part(0), column_part(1))

    stores = [
        pltpu.make_async_copy(nf_v.at[zh], new_first, load_sem.at[5]),
        pltpu.make_async_copy(ns_v.at[zh], new_second, load_sem.at[6]),
    ]
    for store in stores:
        store.start()
    for copy in sent:
        copy.wait_send()
    for store in stores:
        store.wait()


def depth_of(bas):
    return bas.shape[4]


def on_device(Y, tokens, grad, basis, first, second):
    held, width = tokens.shape
    cols = grad.shape[1]
    rows, rank = basis.shape
    own = first.shape[0]
    part_b = cols - PART_A
    deep = rank // Z_LO
    y_rows, pair_rows = rank // Y, Z_HI * own
    assert y_rows == X * pair_rows
    scratch = [
        ((held // 2, width), BF16),
        ((held, cols), BF16),
        ((Z_HI, rows, rank), BF16),
        ((Y, X, Z_HI, rows, deep), BF16),
        ((Z_LO, held, deep), BF16),
        ((Z_HI, own, cols), F32),
        ((Z_HI, own, cols), F32),
        ((Z_HI, own, cols), F32),
        ((Z_HI, own, cols), F32),
        ((Y, y_rows, PART_A), F32),
        ((X, Y, pair_rows, part_b), F32),
        ((X, pair_rows, PART_A), F32),
        ((Y, pair_rows, part_b), F32),
        ((pair_rows, PART_A), F32),
        ((pair_rows, part_b), F32),
    ]
    scratch += [((2, Y // 2, y_rows, PART_A), BF16)] * 2
    scratch += [((2, X // 2, pair_rows, PART_A), BF16)] * 2
    scratch += [((2, X // 2, Y, pair_rows, part_b), BF16)] * 2
    scratch += [((2, Y // 2, pair_rows, part_b), BF16)] * 2
    scratch += [((pair_rows, PART_A), BF16)] * 2
    scratch += [((pair_rows, part_b), BF16)] * 2
    scratch += [
        ((Y, X, pair_rows, PART_A), BF16),
        ((Y, X, pair_rows, part_b), BF16),
        ((Z_HI, rows, PART_A), BF16),
        ((Z_HI, rows, part_b), BF16),
        ((Z_LO, CORES, rows, PART_A), BF16),
        ((Z_LO, CORES, rows, part_b), BF16),
    ]
    anywhere = pl.BlockSpec(memory_space=pl.ANY)
    return pl.pallas_call(
        functools.partial(kernel, Y),
        out_shape=(
            jax.ShapeDtypeStruct(first.shape, F32),
            jax.ShapeDtypeStruct(second.shape, F32),
            jax.ShapeDtypeStruct((rows, Z_LO * CORES * cols), BF16),
        ),
        in_specs=[anywhere] * 5,
        out_specs=(anywhere, anywhere, pl.BlockSpec(memory_space=pltpu.VMEM)),
        scratch_shapes=[pltpu.VMEM(shape, dtype) for shape, dtype in scratch]
        + [
            pltpu.SemaphoreType.DMA((COPIES,)),
            pltpu.SemaphoreType.DMA((COPIES,)),
            pltpu.SemaphoreType.DMA((7,)),
        ],
        compiler_params=pltpu.CompilerParams(
            collective_id=0, has_side_effects=True, vmem_limit_bytes=44 * 2**20
        ),
        cost_estimate=pl.CostEstimate(flops=2 * 10**9, bytes_accessed=10**7, transcendentals=0),
    )(tokens, grad, basis, first, second)


def solution(mesh):
    placed = (P("dp", None), P("dp", "fsdp"), P("dp", None), P("dp", "fsdp"), P("dp", "fsdp"))
    Y = mesh.shape["dp"] // (X * Z_HI)
    return jax.shard_map(
        functools.partial(on_device, Y),
        mesh=mesh,
        in_specs=placed,
        out_specs=(P("dp", "fsdp"), P("dp", "fsdp"), P("dp", None)),
        check_vma=False,
    )
```

```python
import functools

import jax
import jax.numpy as jnp
from jax import lax
from jax.experimental import pallas as pl
from jax.experimental.pallas import tpu as pltpu
from jax.sharding import PartitionSpec as P

beta_one = 0.9
beta_two = 0.999
correct_one = 1.0 - 0.9**10
correct_two = 1.0 - 0.999**10

X = 4
Z_HI, Z_LO, CORES = 2, 4, 2
RING = Z_HI * Z_LO
PARTS = ((0, 384), (384, 384), (768, 384), (1152, 224))
LAG = 1
COPIES = 200

MESH = pl.DeviceIdType.MESH
F32, BF16 = jnp.float32, jnp.bfloat16


def wrap(value, n):
    return lax.rem(value + n, n)


def interleave(*steps):
    steps = list(steps)
    while steps:
        steps = [step for step in steps if next(step, "end") != "end"]


def kernel(
    Y, tokens, grad, basis, first, second,
    new_first, new_second, update,
    tok_v, grad_v, basis_v, bas, proj, first_v, second_v, part_refs,
    send_sem, recv_sem, load_sem,
):
    dp, fs = lax.axis_index("dp"), lax.axis_index("fsdp")
    zh, xy = lax.rem(dp, Z_HI), dp // Z_HI
    x, y = lax.rem(xy, X), xy // X
    core, zl = lax.rem(fs, CORES), fs // CORES
    z = zh * Z_LO + zl
    half_tokens = tok_v.shape[0]
    deep = bas.shape[4]
    rows = basis_v.shape[1]
    cols = grad.shape[0]

    def device(y_, x_, z_, core_):
        return ((y_ * X + x_) * Z_HI + z_ // Z_LO, lax.rem(z_, Z_LO) * CORES + core_)

    at_y = lambda t: device(t, x, z, core)
    at_x = lambda t: device(y, t, z, core)
    at_z = lambda t: device(y, x, t, core)
    opposite = wrap(z + Z_LO - RING, RING)
    sibling = device(y, x, z, 1 - core)
    partner = at_z(opposite)

    sent = []

    def send(src, dst, target):
        k = len(sent)
        copy = pltpu.make_async_remote_copy(
            src_ref=src, dst_ref=dst, send_sem=send_sem.at[k], recv_sem=recv_sem.at[k],
            device_id=target, device_id_type=MESH,
        )
        copy.start()
        sent.append(copy)
        return copy

    def ring_gather(n, pos, target, block, half):
        flying = {}
        for s in range(n // 2):
            for d, h in ((1, 0), (-1, 1)):
                t = wrap(pos - d * s, n)
                if s:
                    flying[d].wait_recv()
                ref = block(t) if s < n // 2 - 1 else half(t, h)
                flying[d] = send(ref, ref, target(wrap(pos + d, n)))
            yield
        for copy in flying.values():
            copy.wait_recv()

    def ring_scatter(pos, target, own, sbuf, rbuf, result):
        size = own.shape[1] // 2
        halves = (pl.ds(0, size), pl.ds(size, size))
        far, first_half, second_half = wrap(pos + 2 - X, X), {}, {}
        for i, d in ((0, 1), (1, -1)):
            t = wrap(pos + d, X)
            mine, other = halves[i], halves[1 - i]
            sbuf[i, 0, mine] = own[far, mine].astype(BF16)
            first_half[i] = send(sbuf.at[i, 0, mine], rbuf.at[i, 0, mine], target(t))
            sbuf[i, 1, other] = own[t, other].astype(BF16)
            second_half[i] = send(sbuf.at[i, 1, other], rbuf.at[i, 1, other], target(t))
        yield
        for i, d in ((0, 1), (1, -1)):
            t, mine = wrap(pos + d, X), halves[i]
            first_half[i].wait_recv()
            sbuf[i, 1, mine] = (own[t, mine] + rbuf[i, 0, mine].astype(F32)).astype(BF16)
            first_half[i] = send(sbuf.at[i, 1, mine], rbuf.at[i, 1, mine], target(t))
        yield
        total = own[pos]
        for i in (0, 1):
            second_half[i].wait_recv()
            first_half[i].wait_recv()
            total = total + rbuf[i, 1].astype(F32)
        result[...] = total

    def direct_gather(n, pos, target, block):
        flying = []
        for k in nearest(n):
            flying.append(send(block(pos), block(pos), target(wrap(pos + k, n))))
        yield
        for copy in flying:
            copy.wait_recv()

    def direct_scatter(n, pos, target, own, sbuf, rbuf, result):
        flying = []
        for i, k in enumerate(nearest(n)):
            t = wrap(pos + k, n)
            sbuf[i] = own[t].astype(BF16)
            flying.append(send(sbuf.at[i], rbuf.at[i], target(t)))
        yield
        total = own[pos]
        for i, copy in enumerate(flying):
            copy.wait_recv()
            total = total + rbuf[i].astype(F32)
        result[...] = total.reshape(result.shape)

    loads = [
        pltpu.make_async_copy(basis, basis_v.at[zh], load_sem.at[0]),
        pltpu.make_async_copy(first, first_v.at[zh], load_sem.at[1]),
        pltpu.make_async_copy(second, second_v.at[zh], load_sem.at[2]),
        pltpu.make_async_copy(tokens.at[pl.ds(core * half_tokens, half_tokens)], tok_v, load_sem.at[3]),
        pltpu.make_async_copy(grad, grad_v, load_sem.at[4]),
    ]
    for load in loads:
        load.start()

    barrier = pltpu.get_barrier_semaphore()
    near = [at_z(wrap(z + k - RING, RING)) for k in range(1, RING)] + [sibling]
    near += [at_x(wrap(x + k, X)) for k in nearest(X)]
    for k in nearest(Y):
        t = wrap(y + k, Y)
        near += [at_y(t), device(t, x, opposite, core)]
    for target in near:
        pl.semaphore_signal(barrier, inc=1, device_id=target, device_id_type=MESH)

    loads[0].wait()
    share = pl.ds(core * (rows // 2), rows // 2)
    bas[y, x, zh, share] = basis_v[zh, share, pl.ds(zl * deep, deep)]
    pl.semaphore_wait(barrier, len(near))
    ref = bas.at[y, x, zh, share]
    columns = {0: [send(ref, ref, partner)]}
    for k in nearest(Y):
        t = wrap(y + k, Y)
        columns[k] = [send(ref, ref, at_y(t)), send(ref, ref, device(t, x, opposite, core))]
    across = {}
    for k in columns:
        for copy in columns[k]:
            copy.wait_recv()
        ref = bas.at[wrap(y - k, Y), x, :, share]
        across[k] = [send(ref, ref, at_x(wrap(x + j, X))) for j in nearest(X)]
    loads[1].wait()
    loads[2].wait()
    to_sibling = {}
    for k in across:
        for copy in across[k]:
            copy.wait_recv()
        ref = bas.at[wrap(y - k, Y), :, :, share]
        to_sibling[k] = send(ref, ref, sibling)

    loads[3].wait()
    inner = X * Z_HI * rows
    total = jnp.zeros((half_tokens, deep), F32)
    for k in to_sibling:
        to_sibling[k].wait_recv()
        t = wrap(y - k, Y)
        total += jnp.dot(
            tok_v[:, pl.ds(pl.multiple_of(t * inner, inner), inner)], bas[t].reshape(inner, deep),
            preferred_element_type=F32,
        )
    mine = pl.ds(core * half_tokens, half_tokens)
    proj[zl, mine] = total.astype(BF16)
    ref = proj.at[zl, mine]
    along = [send(ref, ref, at_z(zh * Z_LO + wrap(zl + k - Z_LO, Z_LO))) for k in range(1, Z_LO)]
    beside = [send(ref, ref, sibling)]
    loads[4].wait()
    for k in range(Z_LO):
        r = wrap(zl - k, Z_LO)
        if k:
            along[k - 1].wait_recv()
            ref = proj.at[r, mine]
            beside.append(send(ref, ref, sibling))
        beside[k].wait_recv()
        turned = proj[r].T
        for (low, width), refs in zip(PARTS, part_refs, strict=True):
            own = refs[0]
            part = lax.dot_general(
                turned, grad_v[pl.ds(low, width)], (((1,), (1,)), ((), ())), preferred_element_type=F32
            )
            high = own.shape[2]
            per = deep // (X * high)
            part = part.reshape(per, X, high, width)
            for t in range(X):
                own[t, pl.ds(r * per, per)] = part[:, t]

    pairs = [send(ref, ref, partner) for ref in (first_v.at[zh], second_v.at[zh], basis_v.at[zh])]
    waiting = list(pairs)

    def column_part(number):
        low, width = PARTS[number]
        own, sbuf, rbuf, mid, sbuf2, rbuf2, total, pair_s, pair_r, whole, out_s, out_r = part_refs[number]
        for _ in range(number * LAG):
            yield
        yield from ring_scatter(x, at_x, own, sbuf, rbuf, mid)
        yield from direct_scatter(Y, y, at_y, mid, sbuf2, rbuf2, total)
        pair_s[...] = total[...].astype(BF16)
        copy = send(pair_s, pair_r, partner)
        yield
        copy.wait_recv()
        while waiting:
            waiting.pop().wait_recv()
        low_grad = total[...] + pair_r[...].astype(F32)
        span = pl.ds(low, width)
        old_first = first_v[:, :, span].reshape(low_grad.shape)
        old_second = second_v[:, :, span].reshape(low_grad.shape)
        fresh_first = beta_one * old_first + (1.0 - beta_one) * low_grad
        fresh_second = beta_two * old_second + (1.0 - beta_two) * low_grad * low_grad
        direction = (
            fresh_first / correct_one / (jnp.sqrt(fresh_second / correct_two) + 1e-08)
        ).astype(BF16)
        whole[y, x] = direction
        below = new_first.shape[0]
        new_first[:, span] = jnp.where(zh == 0, fresh_first[:below], fresh_first[below:])
        new_second[:, span] = jnp.where(zh == 0, fresh_second[:below], fresh_second[below:])
        yield from direct_gather(Y, y, at_y, lambda t: whole.at[t, x])
        yield from ring_gather(
            X, x, at_x, lambda t: whole.at[:, t],
            lambda t, h: whole.at[pl.ds(h * (Y // 2), Y // 2), t],
        )
        block = jnp.dot(
            basis_v[...].reshape(Z_HI * rows, -1), whole[...].reshape(-1, width),
            preferred_element_type=F32,
        ).astype(BF16)
        out_s[...] = block.reshape(out_s.shape)
        moving = {}
        for step in (1, -1):
            to = wrap(z + step, RING)
            moving[step] = send(out_s.at[to // Z_LO], out_r.at[zl, core], at_z(to))
        for step in (2, -2):
            to = wrap(z + step, RING)
            cut = pl.ds(0 if step > 0 else rows // 2, rows // 2)
            moving[step] = send(out_s.at[to // Z_LO, cut], out_r.at[zl, core, cut], at_z(to))
        out_r[zl, core] = out_s[zh]
        beside = [send(out_r.at[zl, core], out_r.at[zl, core], sibling)]
        yield
        for step in (1, -1):
            moving[step].wait_recv()
            ref = out_r.at[wrap(zl - step, Z_LO), core]
            beside.append(send(ref, ref, sibling))
        yield
        moving[2].wait_recv()
        moving[-2].wait_recv()
        ref = out_r.at[wrap(zl + 2, Z_LO), core]
        beside.append(send(ref, ref, sibling))
        yield
        for copy in beside:
            copy.wait_recv()
        for block in range(Z_LO):
            for c in range(CORES):
                at = (block * CORES + c) * cols + low
                update[:, at : at + width] = out_r[block, c]

    interleave(*[column_part(number) for number in range(len(PARTS))])

    for copy in sent:
        copy.wait_send()


def nearest(n):
    return sorted((k for k in range(1 - n // 2, n // 2 + 1) if k), key=abs)


def part_scratch(Y, rank, rows, pair_rows, width):
    block = (Y, pair_rows, width)
    bulk = [((X, *block), F32)] + [((2, 2, *block), BF16)] * 2
    rest = [(block, F32)] + [((Y - 1, pair_rows, width), BF16)] * 2
    return bulk + rest + [
        ((pair_rows, width), F32),
        ((pair_rows, width), BF16),
        ((pair_rows, width), BF16),
        ((Y, X, pair_rows, width), BF16),
        ((Z_HI, rows, width), BF16),
        ((Z_LO, CORES, rows, width), BF16),
    ]


def on_device(Y, tokens, grad, basis, first, second):
    held, width = tokens.shape
    cols = grad.shape[1]
    rows, rank = basis.shape
    own = first.shape[0]
    deep = rank // Z_LO
    scratch = [
        ((held // 2, width), BF16),
        ((cols, held), BF16),
        ((Z_HI, rows, rank), BF16),
        ((Y, X, Z_HI, rows, deep), BF16),
        ((Z_LO, held, deep), BF16),
        ((Z_HI, own, cols), F32),
        ((Z_HI, own, cols), F32),
        [part_scratch(Y, rank, rows, Z_HI * own, wide) for _, wide in PARTS],
    ]

    def placed(item):
        return [placed(one) for one in item] if isinstance(item, list) else pltpu.VMEM(*item)

    return pl.pallas_call(
        functools.partial(kernel, Y),
        out_shape=(
            jax.ShapeDtypeStruct(first.shape, F32),
            jax.ShapeDtypeStruct(second.shape, F32),
            jax.ShapeDtypeStruct((rows, Z_LO * CORES * cols), BF16),
        ),
        in_specs=[pl.BlockSpec(memory_space=pltpu.HBM)] * 5,
        out_specs=(pl.BlockSpec(memory_space=pltpu.VMEM),) * 3,
        scratch_shapes=placed(scratch)
        + [
            pltpu.SemaphoreType.DMA((COPIES,)),
            pltpu.SemaphoreType.DMA((COPIES,)),
            pltpu.SemaphoreType.DMA((5,)),
        ],
        compiler_params=pltpu.CompilerParams(
            collective_id=0, has_side_effects=True, vmem_limit_bytes=51 * 2**20
        ),
        cost_estimate=pl.CostEstimate(flops=2 * 10**9, bytes_accessed=10**7, transcendentals=0),
    )(tokens, grad.T, basis, first, second)


def solution(mesh):
    placed = (P("dp", None), P("dp", "fsdp"), P("dp", None), P("dp", "fsdp"), P("dp", "fsdp"))
    Y = mesh.shape["dp"] // (X * Z_HI)
    return jax.shard_map(
        functools.partial(on_device, Y),
        mesh=mesh,
        in_specs=placed,
        out_specs=(P("dp", "fsdp"), P("dp", "fsdp"), P("dp", None)),
        check_vma=False,
    )
```

```python
import functools
import itertools

import jax
import jax.numpy as jnp
from jax import lax
from jax.experimental import pallas as pl
from jax.experimental.pallas import tpu as pltpu
from jax.sharding import PartitionSpec as P

beta_one = 0.9
beta_two = 0.999
correct_one = 1.0 - 0.9**10
correct_two = 1.0 - 0.999**10

X = 4
Z_HI, Z_LO, CORES = 2, 4, 2
RING = Z_HI * Z_LO
PARTS = ((0, 512, "y"), (512, 512, "x"), (1024, 352, "x"))
COPIES = 67

MESH = pl.DeviceIdType.MESH
F32, BF16 = jnp.float32, jnp.bfloat16


def wrap(value, n):
    return lax.rem(value + n, n)


def interleave(*steps):
    steps = list(steps)
    while steps:
        steps = [step for step in steps if next(step, "end") != "end"]


def kernel(
    Y, tokens, grad, basis, first, second,
    own_grad, blocks,
    tok_v, grad_v, basis_v, bas, proj, first_v, second_v, grad_sum,
    own, sbuf, rbuf, mid, row_s, row_r, pair_s, pair_r, part_refs,
    send_sem, recv_sem, load_sem,
):
    dp, fs = lax.axis_index("dp"), lax.axis_index("fsdp")
    zh, xy = lax.rem(dp, Z_HI), dp // Z_HI
    x, y = lax.rem(xy, X), xy // X
    core, zl = lax.rem(fs, CORES), fs // CORES
    z = zh * Z_LO + zl
    half_tokens = tok_v.shape[0]
    deep = bas.shape[4]
    rows = basis_v.shape[1]
    cols = grad.shape[0]

    def device(y_, x_, z_, core_):
        return ((y_ * X + x_) * Z_HI + z_ // Z_LO, lax.rem(z_, Z_LO) * CORES + core_)

    at_y = lambda t: device(t, x, z, core)
    at_x = lambda t: device(y, t, z, core)
    at_z = lambda t: device(y, x, t, core)
    opposite = wrap(z + Z_LO - RING, RING)
    sibling = device(y, x, z, 1 - core)
    partner = at_z(opposite)

    sent, lanes = [], itertools.count()

    def send(src, dst, target, lane=None):
        k = next(lanes) if lane is None else lane
        copy = pltpu.make_async_remote_copy(
            src_ref=src, dst_ref=dst, send_sem=send_sem.at[k], recv_sem=recv_sem.at[k],
            device_id=target, device_id_type=MESH,
        )
        copy.start()
        if lane is None:
            sent.append(copy)
        return copy

    def joint(lane, whole):
        copy = pltpu.make_async_remote_copy(
            src_ref=whole, dst_ref=whole, send_sem=send_sem.at[lane], recv_sem=recv_sem.at[lane],
            device_id=sibling, device_id_type=MESH,
        )
        sent.append(copy)
        return copy

    def ring_gather(n, pos, target, block, half):
        flying = [send(block(pos), block(pos), target(wrap(pos + d, n))) for d in (1, -1)]
        for s in range(1, n // 2):
            yield
            if n == X:
                yield
            lane = next(lanes) if s == n // 2 - 1 else None
            for i, d in ((0, 1), (1, -1)):
                flying[i].wait_recv()
                t = wrap(pos - d * s, n)
                if s < n // 2 - 1:
                    flying[i] = send(block(t), block(t), target(wrap(pos + d, n)))
                else:
                    send(half(t, i), half(t, i), target(wrap(pos + d, n)), lane)
        both = joint(lane, block(wrap(pos + n // 2 - n, n)))
        yield
        both.wait_recv()

    def direct_scatter(pos, target, own, sbuf, rbuf, result):
        lane = next(lanes)
        for i, k in enumerate(nearest(X)):
            t = wrap(pos + k, X)
            sbuf[i] = own[t].astype(BF16)
            send(sbuf.at[i], rbuf.at[i], target(t), lane)
        every = joint(lane, rbuf)
        yield
        total = own[pos]
        every.wait_recv()
        for i in range(X - 1):
            total = total + rbuf[i].astype(F32)
        result[...] = total

    def direct_gather(n, pos, target, block, others):
        lane = next(lanes)
        for k in nearest(n):
            send(block(pos), block(pos), target(wrap(pos + k, n)), lane)
        every = joint(lane, others)
        yield
        if n == Y:
            yield
        every.wait_recv()

    loads = [
        pltpu.make_async_copy(basis, basis_v.at[zh], load_sem.at[0]),
        pltpu.make_async_copy(first, first_v.at[zh], load_sem.at[1]),
        pltpu.make_async_copy(second, second_v.at[zh], load_sem.at[2]),
        pltpu.make_async_copy(tokens.at[pl.ds(core * half_tokens, half_tokens)], tok_v, load_sem.at[3]),
        pltpu.make_async_copy(grad, grad_v, load_sem.at[4]),
    ]
    for load in loads:
        load.start()

    barrier = pltpu.get_barrier_semaphore()
    near = [at_z(wrap(z + k - RING, RING)) for k in range(1, RING)] + [sibling]
    near += [at_x(wrap(x + k, X)) for k in nearest(X)]
    for k in nearest(Y):
        t = wrap(y + k, Y)
        near += [at_y(t), device(t, x, opposite, core)]
    for target in near:
        pl.semaphore_signal(barrier, inc=1, device_id=target, device_id_type=MESH)

    loads[0].wait()
    share = pl.ds(core * (rows // 2), rows // 2)
    rank, y_rows = basis_v.shape[2], basis_v.shape[2] // Y
    column = lax.broadcasted_iota(jnp.int32, (rank, deep), 1)
    wanted = (zl + Z_LO * (column // y_rows)) * y_rows + lax.rem(column, y_rows)
    picks = (lax.broadcasted_iota(jnp.int32, (rank, deep), 0) == wanted).astype(BF16)
    bas[y, x, zh, share] = jnp.dot(
        basis_v[zh, share], picks, preferred_element_type=F32
    ).astype(BF16)
    pl.semaphore_wait(barrier, len(near))
    ref = bas.at[y, x, zh, share]
    columns = {0: send(ref, ref, partner)}
    for k in nearest(Y):
        t = wrap(y + k, Y)
        lane = next(lanes)
        send(ref, ref, at_y(t), lane)
        send(ref, ref, device(t, x, opposite, core), lane)
        columns[k] = joint(lane, bas.at[t, x, :, share])
    across = {}
    for k in columns:
        columns[k].wait_recv()
        ref = bas.at[wrap(y - k, Y), x, :, share]
        lane = next(lanes)
        for j in nearest(X):
            send(ref, ref, at_x(wrap(x + j, X)), lane)
        across[k] = joint(lane, bas.at[wrap(y - k, Y), pl.ds(0, X - 1), :, share])
    to_sibling = {}
    for k in across:
        across[k].wait_recv()
        ref = bas.at[wrap(y - k, Y), :, :, share]
        to_sibling[k] = send(ref, ref, sibling)

    loads[3].wait()
    inner = X * Z_HI * rows
    total = jnp.zeros((half_tokens, deep), F32)
    for k in to_sibling:
        to_sibling[k].wait_recv()
        t = wrap(y - k, Y)
        total += jnp.dot(
            tok_v[:, pl.ds(pl.multiple_of(t * inner, inner), inner)], bas[t].reshape(inner, deep),
            preferred_element_type=F32,
        )
    mine = pl.ds(core * half_tokens, half_tokens)
    proj[zl, mine] = total.astype(BF16)
    ref = proj.at[zl, mine]
    along = [next(lanes) for _ in range(1, Z_LO)]
    for k in range(1, Z_LO):
        send(ref, ref, at_z(zh * Z_LO + wrap(zl + k - Z_LO, Z_LO)), along[k - 1])
    for lane in along:
        joint(lane, ref)
    beside = [send(ref, ref, sibling)]
    loads[4].wait()
    high = own.shape[3]
    per = deep // (X * high)
    row_lane = next(lanes)

    def rank_slice(k, r):
        yield from direct_scatter(x, at_x, own.at[k], sbuf.at[k], rbuf.at[k], mid.at[r])
        for j in range(per):
            t = r + j * Z_LO
            row_s[t] = mid[r, j].astype(BF16)

            @pl.when(t != y)
            def _():
                send(row_s.at[t], row_r.at[y], at_y(t), row_lane)

    def advance(steps):
        steps[:] = [step for step in steps if next(step, "end") != "end"]

    summing = []
    for k in range(Z_LO):
        r = zl
        if k:
            far = 1 + lax.rem(k - 1 + y, Z_LO - 1)
            r = wrap(zl - far, Z_LO)
            ref = proj.at[r, mine]
            pltpu.make_async_remote_copy(
                src_ref=ref, dst_ref=ref, send_sem=send_sem.at[along[0] + far - 1],
                recv_sem=recv_sem.at[along[0] + far - 1], device_id=sibling, device_id_type=MESH,
            ).wait_recv()
            beside.append(send(ref, ref, sibling))
        beside[k].wait_recv()
        part = lax.dot_general(
            proj[r].T, grad_v[...], (((1,), (1,)), ((), ())), preferred_element_type=F32
        ).reshape(per, X, high, cols)
        for t in range(X):
            own[k, t] = part[:, t]
        summing.insert(0, rank_slice(k, r))
        advance(summing)
    loads[1].wait()
    loads[2].wait()
    lane = next(lanes)
    for ref in (first_v.at[zh], second_v.at[zh]):
        send(ref, ref, partner, lane)
    moments = joint(lane, first_v)
    while summing:
        advance(summing)
    row_sums = joint(row_lane, row_r.at[pl.ds(0, Y - 1)])

    total = mid[lax.rem(y, Z_LO), y // Z_LO]
    row_sums.wait_recv()
    for k in nearest(Y):
        total = total + row_r[wrap(y + k, Y)].astype(F32)
    pair_s[...] = total.astype(BF16)
    copy = send(pair_s, pair_r, partner)
    basis_pair = [send(basis_v.at[zh], basis_v.at[zh], partner)]
    moments.wait_recv()
    copy.wait_recv()
    low_grad = total + pair_r[...].astype(F32)
    fresh_first = beta_one * first_v[...].reshape(low_grad.shape) + (1.0 - beta_one) * low_grad
    fresh_second = (
        beta_two * second_v[...].reshape(low_grad.shape) + (1.0 - beta_two) * low_grad * low_grad
    )
    direction = (
        fresh_first / correct_one / (jnp.sqrt(fresh_second / correct_two) + 1e-08)
    ).astype(BF16)
    below = grad_sum.shape[0]
    grad_sum[...] = jnp.where(zh == 0, low_grad[:below], low_grad[below:])
    store = pltpu.make_async_copy(grad_sum, own_grad, load_sem.at[5 + len(PARTS)])
    store.start()
    stores = [store]
    for (low, width, _), refs in zip(PARTS, part_refs, strict=True):
        refs[0][y, x] = direction[:, low : low + width]

    def column_part(number):
        low, width, way = PARTS[number]
        whole, out_s, out_r = part_refs[number]
        if way == "y":
            yield from direct_gather(
                X, x, at_x, lambda t: whole.at[y, t], whole.at[y, pl.ds(0, X - 1)]
            )
            yield from ring_gather(
                Y, y, at_y, lambda t: whole.at[t],
                lambda t, h: whole.at[t, pl.ds(h * (X // 2), X // 2)],
            )
        else:
            yield from direct_gather(
                Y, y, at_y, lambda t: whole.at[t, x], whole.at[pl.ds(0, Y - 1), x]
            )
            yield from ring_gather(
                X, x, at_x, lambda t: whole.at[:, t],
                lambda t, h: whole.at[pl.ds(h * (Y // 2), Y // 2), t],
            )
        while basis_pair:
            basis_pair.pop().wait_recv()
        block = jnp.dot(
            basis_v[...].reshape(Z_HI * rows, -1), whole[...].reshape(-1, width),
            preferred_element_type=F32,
        ).astype(BF16)
        out_s[...] = block.reshape(out_s.shape)
        moving = {}
        for step in (1, -1):
            to = wrap(z + step, RING)
            moving[step] = send(out_s.at[to // Z_LO], out_r.at[zl, core], at_z(to))
        lane = next(lanes)
        for step in (2, -2):
            to = wrap(z + step, RING)
            cut = pl.ds(0 if step > 0 else rows // 2, rows // 2)
            send(out_s.at[to // Z_LO, cut], out_r.at[zl, core, cut], at_z(to), lane)
        far = out_r.at[wrap(zl + 2 - Z_LO, Z_LO), core]
        moving[2] = joint(lane, far)
        out_r[zl, core] = out_s[zh]
        lane = next(lanes)
        send(out_r.at[zl, core], out_r.at[zl, core], sibling, lane)
        yield
        for step in (1, -1):
            moving[step].wait_recv()
            ref = out_r.at[wrap(zl - step, Z_LO), core]
            send(ref, ref, sibling, lane)
        yield
        moving[2].wait_recv()
        send(far, far, sibling, lane)
        beside = joint(lane, out_r.at[:, 1 - core])
        yield
        beside.wait_recv()
        store = pltpu.make_async_copy(out_r, blocks[number], load_sem.at[5 + number])
        store.start()
        stores.append(store)

    interleave(*[column_part(number) for number in range(len(PARTS))])
    used = next(lanes)
    assert used == COPIES, used

    for copy in sent:
        copy.wait_send()
    for store in stores:
        store.wait()


def finish(own_grad, first, second, blocks, new_first, new_second, update):
    low_grad = own_grad[...]
    new_first[...] = beta_one * first[...] + (1.0 - beta_one) * low_grad
    new_second[...] = beta_two * second[...] + (1.0 - beta_two) * low_grad * low_grad
    cols = first.shape[1]
    for (low, width, _), part in zip(PARTS, blocks, strict=True):
        for block in range(Z_LO):
            for c in range(CORES):
                at = (block * CORES + c) * cols + low
                update[:, at : at + width] = part[block, c]


def nearest(n):
    return sorted((k for k in range(1 - n // 2, n // 2 + 1) if k), key=abs)


def on_device(Y, tokens, grad, basis, first, second):
    held, width = tokens.shape
    cols = grad.shape[1]
    rows, rank = basis.shape
    own = first.shape[0]
    deep = rank // Z_LO
    per, pair_rows = Y // Z_LO, Z_HI * own
    scratch = [
        ((held // 2, width), BF16),
        ((cols, held), BF16),
        ((Z_HI, rows, rank), BF16),
        ((Y, X, Z_HI, rows, deep), BF16),
        ((Z_LO, held, deep), BF16),
        ((Z_HI, own, cols), F32),
        ((Z_HI, own, cols), F32),
        ((own, cols), F32),
        ((Z_LO, X, per, pair_rows, cols), F32),
        ((Z_LO, X - 1, per, pair_rows, cols), BF16),
        ((Z_LO, X - 1, per, pair_rows, cols), BF16),
        ((Z_LO, per, pair_rows, cols), F32),
        ((Y, pair_rows, cols), BF16),
        ((Y, pair_rows, cols), BF16),
        ((pair_rows, cols), BF16),
        ((pair_rows, cols), BF16),
        [
            [
                ((Y, X, pair_rows, wide), BF16),
                ((Z_HI, rows, wide), BF16),
                ((Z_LO, CORES, rows, wide), BF16),
            ]
            for _, wide, _ in PARTS
        ],
    ]

    def placed(item):
        return [placed(one) for one in item] if isinstance(item, list) else pltpu.VMEM(*item)

    placed_blocks = [jax.ShapeDtypeStruct((Z_LO, CORES, rows, wide), BF16) for _, wide, _ in PARTS]
    anywhere = pl.BlockSpec(memory_space=pl.ANY)
    own_grad, blocks = pl.pallas_call(
        functools.partial(kernel, Y),
        out_shape=(jax.ShapeDtypeStruct(first.shape, F32), placed_blocks),
        in_specs=[anywhere] * 5,
        out_specs=(anywhere, [anywhere] * len(PARTS)),
        scratch_shapes=placed(scratch)
        + [
            pltpu.SemaphoreType.DMA((COPIES,)),
            pltpu.SemaphoreType.DMA((COPIES,)),
            pltpu.SemaphoreType.DMA((6 + len(PARTS),)),
        ],
        compiler_params=pltpu.CompilerParams(
            collective_id=0, has_side_effects=True, vmem_limit_bytes=56 * 2**20
        ),
        cost_estimate=pl.CostEstimate(flops=2 * 10**9, bytes_accessed=10**7, transcendentals=0),
    )(tokens, grad.T, basis, first, second)
    high = 16
    whole = pl.BlockSpec(first.shape, lambda i: (0, 0))
    return pl.pallas_call(
        finish,
        grid=(rows // high,),
        out_shape=(
            jax.ShapeDtypeStruct(first.shape, F32),
            jax.ShapeDtypeStruct(second.shape, F32),
            jax.ShapeDtypeStruct((rows, Z_LO * CORES * cols), BF16),
        ),
        in_specs=[
            whole, whole, whole,
            [pl.BlockSpec((Z_LO, CORES, high, wide), lambda i: (0, 0, i, 0)) for _, wide, _ in PARTS],
        ],
        out_specs=(whole, whole, pl.BlockSpec((high, Z_LO * CORES * cols), lambda i: (i, 0))),
        compiler_params=pltpu.CompilerParams(vmem_limit_bytes=56 * 2**20),
        cost_estimate=pl.CostEstimate(flops=10**5, bytes_accessed=3 * 10**6, transcendentals=0),
    )(own_grad, first, second, blocks)


def solution(mesh):
    placed = (P("dp", None), P("dp", "fsdp"), P("dp", None), P("dp", "fsdp"), P("dp", "fsdp"))
    Y = mesh.shape["dp"] // (X * Z_HI)
    return jax.shard_map(
        functools.partial(on_device, Y),
        mesh=mesh,
        in_specs=placed,
        out_specs=(P("dp", "fsdp"), P("dp", "fsdp"), P("dp", None)),
        check_vma=False,
    )
```

```python
import functools
import itertools

import jax
import jax.numpy as jnp
from jax import lax
from jax.experimental import pallas as pl
from jax.experimental.pallas import tpu as pltpu
from jax.sharding import PartitionSpec as P

beta_one = 0.9
beta_two = 0.999
correct_one = 1.0 - 0.9**10
correct_two = 1.0 - 0.999**10

X = 4
Z_HI, Z_LO, CORES = 2, 4, 2
RING = Z_HI * Z_LO
PARTS = ((0, 512, "y"), (512, 512, "x"), (1024, 352, "x"))
COPIES = 67

MESH = pl.DeviceIdType.MESH
F32, BF16 = jnp.float32, jnp.bfloat16


def wrap(value, n):
    return lax.rem(value + n, n)


def interleave(*steps):
    steps = list(steps)
    while steps:
        steps = [step for step in steps if next(step, "end") != "end"]


def kernel(
    Y, tokens, grad, basis, first, second,
    own_grad, blocks,
    tok_v, grad_v, basis_v, bas, proj, first_v, second_v, grad_sum,
    own, sbuf, rbuf, mid, row_s, row_r, pair_s, pair_r, part_refs,
    send_sem, recv_sem, load_sem,
):
    dp, fs = lax.axis_index("dp"), lax.axis_index("fsdp")
    zh, xy = lax.rem(dp, Z_HI), dp // Z_HI
    x, y = lax.rem(xy, X), xy // X
    core, zl = lax.rem(fs, CORES), fs // CORES
    z = zh * Z_LO + zl
    half_tokens = tok_v.shape[0]
    deep = bas.shape[4]
    rows = basis_v.shape[1]
    cols = grad.shape[0]

    def device(y_, x_, z_, core_):
        return ((y_ * X + x_) * Z_HI + z_ // Z_LO, lax.rem(z_, Z_LO) * CORES + core_)

    at_y = lambda t: device(t, x, z, core)
    at_x = lambda t: device(y, t, z, core)
    at_z = lambda t: device(y, x, t, core)
    opposite = wrap(z + Z_LO - RING, RING)
    sibling = device(y, x, z, 1 - core)
    partner = at_z(opposite)

    sent, lanes = [], itertools.count()

    def send(src, dst, target, lane=None):
        k = next(lanes) if lane is None else lane
        copy = pltpu.make_async_remote_copy(
            src_ref=src, dst_ref=dst, send_sem=send_sem.at[k], recv_sem=recv_sem.at[k],
            device_id=target, device_id_type=MESH,
        )
        copy.start()
        if lane is None:
            sent.append(copy)
        return copy

    def joint(lane, whole):
        copy = pltpu.make_async_remote_copy(
            src_ref=whole, dst_ref=whole, send_sem=send_sem.at[lane], recv_sem=recv_sem.at[lane],
            device_id=sibling, device_id_type=MESH,
        )
        sent.append(copy)
        return copy

    def ring_gather(n, pos, target, block, half):
        flying = [send(block(pos), block(pos), target(wrap(pos + d, n))) for d in (1, -1)]
        for s in range(1, n // 2):
            yield
            if n == X:
                yield
            lane = next(lanes) if s == n // 2 - 1 else None
            for i, d in ((0, 1), (1, -1)):
                flying[i].wait_recv()
                t = wrap(pos - d * s, n)
                if s < n // 2 - 1:
                    flying[i] = send(block(t), block(t), target(wrap(pos + d, n)))
                else:
                    send(half(t, i), half(t, i), target(wrap(pos + d, n)), lane)
        both = joint(lane, block(wrap(pos + n // 2 - n, n)))
        yield
        both.wait_recv()

    def direct_scatter(pos, target, own, sbuf, rbuf, result):
        lane = next(lanes)
        for i, k in enumerate(nearest(X)):
            t = wrap(pos + k, X)
            sbuf[i] = own[t].astype(BF16)
            send(sbuf.at[i], rbuf.at[i], target(t), lane)
        every = joint(lane, rbuf)
        yield
        total = own[pos]
        every.wait_recv()
        for i in range(X - 1):
            total = total + rbuf[i].astype(F32)
        result[...] = total

    def direct_gather(n, pos, target, block, others):
        lane = next(lanes)
        for k in nearest(n):
            send(block(pos), block(pos), target(wrap(pos + k, n)), lane)
        every = joint(lane, others)
        yield
        if n == Y:
            yield
        every.wait_recv()

    loads = [
        pltpu.make_async_copy(basis, basis_v.at[zh], load_sem.at[0]),
        pltpu.make_async_copy(first, first_v.at[zh], load_sem.at[1]),
        pltpu.make_async_copy(second, second_v.at[zh], load_sem.at[2]),
        pltpu.make_async_copy(tokens.at[pl.ds(core * half_tokens, half_tokens)], tok_v, load_sem.at[3]),
        pltpu.make_async_copy(grad, grad_v, load_sem.at[4]),
    ]
    for load in loads:
        load.start()

    barrier = pltpu.get_barrier_semaphore()
    near = [at_z(wrap(z + k - RING, RING)) for k in range(1, RING)] + [sibling]
    near += [at_x(wrap(x + k, X)) for k in nearest(X)]
    for k in nearest(Y):
        t = wrap(y + k, Y)
        near += [at_y(t), device(t, x, opposite, core)]
    for target in near:
        pl.semaphore_signal(barrier, inc=1, device_id=target, device_id_type=MESH)

    loads[0].wait()
    share = pl.ds(core * (rows // 2), rows // 2)
    rank, y_rows = basis_v.shape[2], basis_v.shape[2] // Y
    column = lax.broadcasted_iota(jnp.int32, (rank, deep), 1)
    wanted = (zl + Z_LO * (column // y_rows)) * y_rows + lax.rem(column, y_rows)
    picks = (lax.broadcasted_iota(jnp.int32, (rank, deep), 0) == wanted).astype(BF16)
    bas[y, x, zh, share] = jnp.dot(
        basis_v[zh, share], picks, preferred_element_type=F32
    ).astype(BF16)
    pl.semaphore_wait(barrier, len(near))
    ref = bas.at[y, x, zh, share]
    columns = {0: send(ref, ref, partner)}
    for k in nearest(Y):
        t = wrap(y + k, Y)
        lane = next(lanes)
        send(ref, ref, at_y(t), lane)
        send(ref, ref, device(t, x, opposite, core), lane)
        columns[k] = joint(lane, bas.at[t, x, :, share])
    across = {}
    for k in columns:
        columns[k].wait_recv()
        ref = bas.at[wrap(y - k, Y), x, :, share]
        lane = next(lanes)
        for j in nearest(X):
            send(ref, ref, at_x(wrap(x + j, X)), lane)
        across[k] = joint(lane, bas.at[wrap(y - k, Y), pl.ds(0, X - 1), :, share])
    to_sibling = {}
    for k in across:
        across[k].wait_recv()
        ref = bas.at[wrap(y - k, Y), :, :, share]
        to_sibling[k] = send(ref, ref, sibling)

    loads[3].wait()
    inner = X * Z_HI * rows
    total = jnp.zeros((half_tokens, deep), F32)
    for k in to_sibling:
        to_sibling[k].wait_recv()
        t = wrap(y - k, Y)
        total += jnp.dot(
            tok_v[:, pl.ds(pl.multiple_of(t * inner, inner), inner)], bas[t].reshape(inner, deep),
            preferred_element_type=F32,
        )
    mine = pl.ds(core * half_tokens, half_tokens)
    proj[zl, mine] = total.astype(BF16)
    ref = proj.at[zl, mine]
    along = [next(lanes) for _ in range(1, Z_LO)]
    for k in range(1, Z_LO):
        send(ref, ref, at_z(zh * Z_LO + wrap(zl + k - Z_LO, Z_LO)), along[k - 1])
    for lane in along:
        joint(lane, ref)
    beside = [send(ref, ref, sibling)]
    loads[4].wait()
    high = own.shape[3]
    per = deep // (X * high)
    row_lane = next(lanes)

    def rank_slice(k, r):
        yield from direct_scatter(x, at_x, own.at[k], sbuf.at[k], rbuf.at[k], mid.at[r])
        for j in range(per):
            t = r + j * Z_LO
            row_s[t] = mid[r, j].astype(BF16)

            @pl.when(t != y)
            def _():
                send(row_s.at[t], row_r.at[y], at_y(t), row_lane)

    summing = []
    for k in range(Z_LO):
        r = zl
        if k:
            far = 1 + lax.rem(k - 1 + y, Z_LO - 1)
            r = wrap(zl - far, Z_LO)
            ref = proj.at[r, mine]
            pltpu.make_async_remote_copy(
                src_ref=ref, dst_ref=ref, send_sem=send_sem.at[along[0] + far - 1],
                recv_sem=recv_sem.at[along[0] + far - 1], device_id=sibling, device_id_type=MESH,
            ).wait_recv()
            beside.append(send(ref, ref, sibling))
        if k == Z_LO - 1:
            loads[1].wait()
            loads[2].wait()
            lane = next(lanes)
            for ref in (first_v.at[zh], second_v.at[zh]):
                send(ref, ref, partner, lane)
            moments = joint(lane, first_v)
        beside[k].wait_recv()
        part = lax.dot_general(
            proj[r].T, grad_v[...], (((1,), (1,)), ((), ())), preferred_element_type=F32
        ).reshape(per, X, high, cols)
        for t in range(X):
            own[k, t] = part[:, t]
        summing.append(rank_slice(k, r))
        next(summing[k])
        if k >= 2:
            next(summing[k - 2], None)
    for step in summing[Z_LO - 2 :]:
        next(step, None)
    row_sums = joint(row_lane, row_r.at[pl.ds(0, Y - 1)])

    total = mid[lax.rem(y, Z_LO), y // Z_LO]
    row_sums.wait_recv()
    for k in nearest(Y):
        total = total + row_r[wrap(y + k, Y)].astype(F32)
    pair_s[...] = total.astype(BF16)
    copy = send(pair_s, pair_r, partner)
    moments.wait_recv()
    copy.wait_recv()
    basis_pair = [send(basis_v.at[zh], basis_v.at[zh], partner)]
    low_grad = total + pair_r[...].astype(F32)
    fresh_first = beta_one * first_v[...].reshape(low_grad.shape) + (1.0 - beta_one) * low_grad
    fresh_second = (
        beta_two * second_v[...].reshape(low_grad.shape) + (1.0 - beta_two) * low_grad * low_grad
    )
    direction = (
        fresh_first / correct_one / (jnp.sqrt(fresh_second / correct_two) + 1e-08)
    ).astype(BF16)
    below = grad_sum.shape[0]
    grad_sum[...] = jnp.where(zh == 0, low_grad[:below], low_grad[below:])
    store = pltpu.make_async_copy(grad_sum, own_grad, load_sem.at[5 + len(PARTS)])
    store.start()
    stores = [store]
    for (low, width, _), refs in zip(PARTS, part_refs, strict=True):
        refs[0][y, x] = direction[:, low : low + width]

    def column_part(number):
        low, width, way = PARTS[number]
        whole, out_s, out_r = part_refs[number]
        if way == "y":
            yield from direct_gather(
                X, x, at_x, lambda t: whole.at[y, t], whole.at[y, pl.ds(0, X - 1)]
            )
            yield from ring_gather(
                Y, y, at_y, lambda t: whole.at[t],
                lambda t, h: whole.at[t, pl.ds(h * (X // 2), X // 2)],
            )
        else:
            yield from direct_gather(
                Y, y, at_y, lambda t: whole.at[t, x], whole.at[pl.ds(0, Y - 1), x]
            )
            yield from ring_gather(
                X, x, at_x, lambda t: whole.at[:, t],
                lambda t, h: whole.at[pl.ds(h * (Y // 2), Y // 2), t],
            )
        while basis_pair:
            basis_pair.pop().wait_recv()
        block = jnp.dot(
            basis_v[...].reshape(Z_HI * rows, -1), whole[...].reshape(-1, width),
            preferred_element_type=F32,
        ).astype(BF16)
        out_s[...] = block.reshape(out_s.shape)
        moving = {}
        for step in (1, -1):
            to = wrap(z + step, RING)
            moving[step] = send(out_s.at[to // Z_LO], out_r.at[zl, core], at_z(to))
        lane = next(lanes)
        for step in (2, -2):
            to = wrap(z + step, RING)
            cut = pl.ds(0 if step > 0 else rows // 2, rows // 2)
            send(out_s.at[to // Z_LO, cut], out_r.at[zl, core, cut], at_z(to), lane)
        far = out_r.at[wrap(zl + 2 - Z_LO, Z_LO), core]
        moving[2] = joint(lane, far)
        out_r[zl, core] = out_s[zh]
        lane = next(lanes)
        send(out_r.at[zl, core], out_r.at[zl, core], sibling, lane)
        yield
        for step in (1, -1):
            moving[step].wait_recv()
            ref = out_r.at[wrap(zl - step, Z_LO), core]
            send(ref, ref, sibling, lane)
        yield
        moving[2].wait_recv()
        send(far, far, sibling, lane)
        beside = joint(lane, out_r.at[:, 1 - core])
        yield
        beside.wait_recv()
        store = pltpu.make_async_copy(out_r, blocks[number], load_sem.at[5 + number])
        store.start()
        stores.append(store)

    interleave(*[column_part(number) for number in range(len(PARTS))])
    used = next(lanes)
    assert used == COPIES, used

    for copy in sent:
        copy.wait_send()
    for store in stores:
        store.wait()


def finish(own_grad, first, second, blocks, new_first, new_second, update):
    low_grad = own_grad[...]
    new_first[...] = beta_one * first[...] + (1.0 - beta_one) * low_grad
    new_second[...] = beta_two * second[...] + (1.0 - beta_two) * low_grad * low_grad
    cols = first.shape[1]
    for (low, width, _), part in zip(PARTS, blocks, strict=True):
        for block in range(Z_LO):
            for c in range(CORES):
                at = (block * CORES + c) * cols + low
                update[:, at : at + width] = part[block, c]


def nearest(n):
    return sorted((k for k in range(1 - n // 2, n // 2 + 1) if k), key=abs)


def on_device(Y, tokens, grad, basis, first, second):
    held, width = tokens.shape
    cols = grad.shape[1]
    rows, rank = basis.shape
    own = first.shape[0]
    deep = rank // Z_LO
    per, pair_rows = Y // Z_LO, Z_HI * own
    scratch = [
        ((held // 2, width), BF16),
        ((cols, held), BF16),
        ((Z_HI, rows, rank), BF16),
        ((Y, X, Z_HI, rows, deep), BF16),
        ((Z_LO, held, deep), BF16),
        ((Z_HI, own, cols), F32),
        ((Z_HI, own, cols), F32),
        ((own, cols), F32),
        ((Z_LO, X, per, pair_rows, cols), F32),
        ((Z_LO, X - 1, per, pair_rows, cols), BF16),
        ((Z_LO, X - 1, per, pair_rows, cols), BF16),
        ((Z_LO, per, pair_rows, cols), F32),
        ((Y, pair_rows, cols), BF16),
        ((Y, pair_rows, cols), BF16),
        ((pair_rows, cols), BF16),
        ((pair_rows, cols), BF16),
        [
            [
                ((Y, X, pair_rows, wide), BF16),
                ((Z_HI, rows, wide), BF16),
                ((Z_LO, CORES, rows, wide), BF16),
            ]
            for _, wide, _ in PARTS
        ],
    ]

    def placed(item):
        return [placed(one) for one in item] if isinstance(item, list) else pltpu.VMEM(*item)

    placed_blocks = [jax.ShapeDtypeStruct((Z_LO, CORES, rows, wide), BF16) for _, wide, _ in PARTS]
    anywhere = pl.BlockSpec(memory_space=pl.ANY)
    own_grad, blocks = pl.pallas_call(
        functools.partial(kernel, Y),
        out_shape=(jax.ShapeDtypeStruct(first.shape, F32), placed_blocks),
        in_specs=[anywhere] * 5,
        out_specs=(anywhere, [anywhere] * len(PARTS)),
        scratch_shapes=placed(scratch)
        + [
            pltpu.SemaphoreType.DMA((COPIES,)),
            pltpu.SemaphoreType.DMA((COPIES,)),
            pltpu.SemaphoreType.DMA((6 + len(PARTS),)),
        ],
        compiler_params=pltpu.CompilerParams(
            collective_id=0, has_side_effects=True, vmem_limit_bytes=56 * 2**20
        ),
        cost_estimate=pl.CostEstimate(flops=2 * 10**9, bytes_accessed=10**7, transcendentals=0),
    )(tokens, grad.T, basis, first, second)
    high = 32
    whole = pl.BlockSpec(first.shape, lambda i: (0, 0))
    return pl.pallas_call(
        finish,
        grid=(rows // high,),
        out_shape=(
            jax.ShapeDtypeStruct(first.shape, F32),
            jax.ShapeDtypeStruct(second.shape, F32),
            jax.ShapeDtypeStruct((rows, Z_LO * CORES * cols), BF16),
        ),
        in_specs=[
            whole, whole, whole,
            [pl.BlockSpec((Z_LO, CORES, high, wide), lambda i: (0, 0, i, 0)) for _, wide, _ in PARTS],
        ],
        out_specs=(whole, whole, pl.BlockSpec((high, Z_LO * CORES * cols), lambda i: (i, 0))),
        compiler_params=pltpu.CompilerParams(vmem_limit_bytes=56 * 2**20),
        cost_estimate=pl.CostEstimate(flops=10**5, bytes_accessed=3 * 10**6, transcendentals=0),
    )(own_grad, first, second, blocks)


def solution(mesh):
    placed = (P("dp", None), P("dp", "fsdp"), P("dp", None), P("dp", "fsdp"), P("dp", "fsdp"))
    Y = mesh.shape["dp"] // (X * Z_HI)
    return jax.shard_map(
        functools.partial(on_device, Y),
        mesh=mesh,
        in_specs=placed,
        out_specs=(P("dp", "fsdp"), P("dp", "fsdp"), P("dp", None)),
        check_vma=False,
    )
```

```python
import functools
import itertools

import jax
import jax.numpy as jnp
from jax import lax
from jax.experimental import pallas as pl
from jax.experimental.pallas import tpu as pltpu
from jax.sharding import PartitionSpec as P

beta_one = 0.9
beta_two = 0.999
correct_one = 1.0 - 0.9**10
correct_two = 1.0 - 0.999**10

X = 4
Z_HI, Z_LO, CORES = 2, 4, 2
RING = Z_HI * Z_LO
PARTS = ((0, 512, "y"), (512, 512, "x"), (1024, 352, "x"))
COPIES = 67

MESH = pl.DeviceIdType.MESH
F32, BF16 = jnp.float32, jnp.bfloat16


def wrap(value, n):
    return lax.rem(value + n, n)


def interleave(*steps):
    steps = list(steps)
    while steps:
        steps = [step for step in steps if next(step, "end") != "end"]


def kernel(
    Y, tokens, grad, basis, first, second,
    own_grad, blocks,
    tok_v, grad_v, basis_v, bas, proj, first_v, second_v, grad_sum, turned,
    own, sbuf, rbuf, mid, row_s, row_r, pair_s, pair_r, part_refs,
    send_sem, recv_sem, load_sem,
):
    dp, fs = lax.axis_index("dp"), lax.axis_index("fsdp")
    zh, xy = lax.rem(dp, Z_HI), dp // Z_HI
    x, y = lax.rem(xy, X), xy // X
    core, zl = lax.rem(fs, CORES), fs // CORES
    z = zh * Z_LO + zl
    half_tokens = tok_v.shape[0]
    deep = bas.shape[4]
    rows = basis_v.shape[1]
    cols = grad.shape[0]

    def device(y_, x_, z_, core_):
        return ((y_ * X + x_) * Z_HI + z_ // Z_LO, lax.rem(z_, Z_LO) * CORES + core_)

    at_y = lambda t: device(t, x, z, core)
    at_x = lambda t: device(y, t, z, core)
    at_z = lambda t: device(y, x, t, core)
    opposite = wrap(z + Z_LO - RING, RING)
    sibling = device(y, x, z, 1 - core)
    partner = at_z(opposite)
    mirror = RING - 1 - z

    sent, lanes = [], itertools.count()

    def send(src, dst, target, lane=None):
        k = next(lanes) if lane is None else lane
        copy = pltpu.make_async_remote_copy(
            src_ref=src, dst_ref=dst, send_sem=send_sem.at[k], recv_sem=recv_sem.at[k],
            device_id=target, device_id_type=MESH,
        )
        copy.start()
        if lane is None:
            sent.append(copy)
        return copy

    def joint(lane, whole):
        copy = pltpu.make_async_remote_copy(
            src_ref=whole, dst_ref=whole, send_sem=send_sem.at[lane], recv_sem=recv_sem.at[lane],
            device_id=sibling, device_id_type=MESH,
        )
        sent.append(copy)
        return copy

    def ring_gather(n, pos, target, block, half):
        flying = [send(block(pos), block(pos), target(wrap(pos + d, n))) for d in (1, -1)]
        for s in range(1, n // 2):
            yield
            if n == X:
                yield
            lane = next(lanes) if s == n // 2 - 1 else None
            for i, d in ((0, 1), (1, -1)):
                flying[i].wait_recv()
                t = wrap(pos - d * s, n)
                if s < n // 2 - 1:
                    flying[i] = send(block(t), block(t), target(wrap(pos + d, n)))
                else:
                    send(half(t, i), half(t, i), target(wrap(pos + d, n)), lane)
        both = joint(lane, block(wrap(pos + n // 2 - n, n)))
        yield
        both.wait_recv()

    def direct_scatter(pos, target, own, sbuf, rbuf, result):
        lane = next(lanes)
        for i, k in enumerate(nearest(X)):
            t = wrap(pos + k, X)
            sbuf[i] = own[t].astype(BF16)
            send(sbuf.at[i], rbuf.at[i], target(t), lane)
        every = joint(lane, rbuf)
        yield
        total = own[pos]
        every.wait_recv()
        for i in range(X - 1):
            total = total + rbuf[i].astype(F32)
        result[...] = total

    def direct_gather(n, pos, target, block, others):
        lane = next(lanes)
        for k in nearest(n):
            send(block(pos), block(pos), target(wrap(pos + k, n)), lane)
        every = joint(lane, others)
        yield
        if n == Y:
            yield
        every.wait_recv()

    loads = [
        pltpu.make_async_copy(basis, basis_v.at[zh], load_sem.at[0]),
        pltpu.make_async_copy(first, first_v.at[zh], load_sem.at[1]),
        pltpu.make_async_copy(second, second_v.at[zh], load_sem.at[2]),
        pltpu.make_async_copy(tokens.at[pl.ds(core * half_tokens, half_tokens)], tok_v, load_sem.at[3]),
        pltpu.make_async_copy(grad, grad_v, load_sem.at[4]),
    ]
    for load in loads:
        load.start()

    barrier = pltpu.get_barrier_semaphore()
    near = [at_z(wrap(z + k - RING, RING)) for k in range(1, RING)] + [sibling]
    near += [at_x(wrap(x + k, X)) for k in nearest(X)]
    for k in nearest(Y):
        t = wrap(y + k, Y)
        near += [at_y(t), device(t, x, mirror, core)]
    for target in near:
        pl.semaphore_signal(barrier, inc=1, device_id=target, device_id_type=MESH)

    loads[0].wait()
    share = pl.ds(core * (rows // 2), rows // 2)
    rank, y_rows = basis_v.shape[2], basis_v.shape[2] // Y
    column = lax.broadcasted_iota(jnp.int32, (rank, deep), 1)
    row = lax.broadcasted_iota(jnp.int32, (rank, deep), 0)

    def slice_of(q):
        wanted = (q + Z_LO * (column // y_rows)) * y_rows + lax.rem(column, y_rows)
        picks = (row == wanted).astype(BF16)
        return jnp.dot(basis_v[zh, share], picks, preferred_element_type=F32).astype(BF16)

    bas[y, x, zh, share] = slice_of(zl)
    turned[...] = slice_of(Z_LO - 1 - zl)
    pl.semaphore_wait(barrier, len(near))
    ref = bas.at[y, x, zh, share]
    columns = {0: send(turned, ref, at_z(mirror))}
    for k in nearest(Y):
        t = wrap(y + k, Y)
        lane = next(lanes)
        send(ref, ref, at_y(t), lane)
        send(turned, ref, device(t, x, mirror, core), lane)
        columns[k] = joint(lane, bas.at[t, x, :, share])
    across = {}
    for k in columns:
        columns[k].wait_recv()
        ref = bas.at[wrap(y - k, Y), x, :, share]
        lane = next(lanes)
        for j in nearest(X):
            send(ref, ref, at_x(wrap(x + j, X)), lane)
        across[k] = joint(lane, bas.at[wrap(y - k, Y), pl.ds(0, X - 1), :, share])
    to_sibling = {}
    for k in across:
        across[k].wait_recv()
        ref = bas.at[wrap(y - k, Y), :, :, share]
        to_sibling[k] = send(ref, ref, sibling)

    loads[3].wait()
    inner = X * Z_HI * rows
    total = jnp.zeros((half_tokens, deep), F32)
    for k in to_sibling:
        to_sibling[k].wait_recv()
        t = wrap(y - k, Y)
        total += jnp.dot(
            tok_v[:, pl.ds(pl.multiple_of(t * inner, inner), inner)], bas[t].reshape(inner, deep),
            preferred_element_type=F32,
        )
    mine = pl.ds(core * half_tokens, half_tokens)
    proj[zl, mine] = total.astype(BF16)
    ref = proj.at[zl, mine]
    along = [next(lanes) for _ in range(1, Z_LO)]
    for k in range(1, Z_LO):
        send(ref, ref, at_z(zh * Z_LO + wrap(zl + k - Z_LO, Z_LO)), along[k - 1])
    for lane in along:
        joint(lane, ref)
    beside = [send(ref, ref, sibling)]
    loads[4].wait()
    high = own.shape[3]
    per = deep // (X * high)
    row_lane = next(lanes)

    def rank_slice(k, r):
        yield from direct_scatter(x, at_x, own.at[k], sbuf.at[k], rbuf.at[k], mid.at[r])
        for j in range(per):
            t = r + j * Z_LO
            row_s[t] = mid[r, j].astype(BF16)

            @pl.when(t != y)
            def _():
                send(row_s.at[t], row_r.at[y], at_y(t), row_lane)

    summing = []
    for k in range(Z_LO):
        r = zl
        if k:
            far = 1 + lax.rem(k - 1 + y, Z_LO - 1)
            r = wrap(zl - far, Z_LO)
            ref = proj.at[r, mine]
            pltpu.make_async_remote_copy(
                src_ref=ref, dst_ref=ref, send_sem=send_sem.at[along[0] + far - 1],
                recv_sem=recv_sem.at[along[0] + far - 1], device_id=sibling, device_id_type=MESH,
            ).wait_recv()
            beside.append(send(ref, ref, sibling))
        if k == Z_LO - 1:
            loads[1].wait()
            loads[2].wait()
            lane = next(lanes)
            for ref in (first_v.at[zh], second_v.at[zh]):
                send(ref, ref, partner, lane)
            moments = joint(lane, first_v)
        beside[k].wait_recv()
        part = lax.dot_general(
            proj[r].T, grad_v[...], (((1,), (1,)), ((), ())), preferred_element_type=F32
        ).reshape(per, X, high, cols)
        for t in range(X):
            own[k, t] = part[:, t]
        summing.append(rank_slice(k, r))
        next(summing[k])
        if k >= 2:
            next(summing[k - 2], None)
    for step in summing[Z_LO - 2 :]:
        next(step, None)
    row_sums = joint(row_lane, row_r.at[pl.ds(0, Y - 1)])

    total = mid[lax.rem(y, Z_LO), y // Z_LO]
    row_sums.wait_recv()
    for k in nearest(Y):
        total = total + row_r[wrap(y + k, Y)].astype(F32)
    pair_s[...] = total.astype(BF16)
    copy = send(pair_s, pair_r, partner)
    moments.wait_recv()
    copy.wait_recv()
    basis_pair = [send(basis_v.at[zh], basis_v.at[zh], partner)]
    low_grad = total + pair_r[...].astype(F32)
    fresh_first = beta_one * first_v[...].reshape(low_grad.shape) + (1.0 - beta_one) * low_grad
    fresh_second = (
        beta_two * second_v[...].reshape(low_grad.shape) + (1.0 - beta_two) * low_grad * low_grad
    )
    direction = (
        fresh_first / correct_one / (jnp.sqrt(fresh_second / correct_two) + 1e-08)
    ).astype(BF16)
    below = grad_sum.shape[0]
    grad_sum[...] = jnp.where(zh == 0, low_grad[:below], low_grad[below:])
    store = pltpu.make_async_copy(grad_sum, own_grad, load_sem.at[5 + len(PARTS)])
    store.start()
    stores = [store]
    for (low, width, _), refs in zip(PARTS, part_refs, strict=True):
        refs[0][y, x] = direction[:, low : low + width]

    def column_part(number):
        low, width, way = PARTS[number]
        whole, out_s, out_r = part_refs[number]
        if way == "y":
            yield from direct_gather(
                X, x, at_x, lambda t: whole.at[y, t], whole.at[y, pl.ds(0, X - 1)]
            )
            yield from ring_gather(
                Y, y, at_y, lambda t: whole.at[t],
                lambda t, h: whole.at[t, pl.ds(h * (X // 2), X // 2)],
            )
        else:
            yield from direct_gather(
                Y, y, at_y, lambda t: whole.at[t, x], whole.at[pl.ds(0, Y - 1), x]
            )
            yield from ring_gather(
                X, x, at_x, lambda t: whole.at[:, t],
                lambda t, h: whole.at[pl.ds(h * (Y // 2), Y // 2), t],
            )
        while basis_pair:
            basis_pair.pop().wait_recv()
        block = jnp.dot(
            basis_v[...].reshape(Z_HI * rows, -1), whole[...].reshape(-1, width),
            preferred_element_type=F32,
        ).astype(BF16)
        out_s[...] = block.reshape(out_s.shape)
        moving = {}
        for step in (1, -1):
            to = wrap(z + step, RING)
            moving[step] = send(out_s.at[to // Z_LO], out_r.at[zl, core], at_z(to))
        lane = next(lanes)
        for step in (2, -2):
            to = wrap(z + step, RING)
            cut = pl.ds(0 if step > 0 else rows // 2, rows // 2)
            send(out_s.at[to // Z_LO, cut], out_r.at[zl, core, cut], at_z(to), lane)
        far = out_r.at[wrap(zl + 2 - Z_LO, Z_LO), core]
        moving[2] = joint(lane, far)
        out_r[zl, core] = out_s[zh]
        lane = next(lanes)
        send(out_r.at[zl, core], out_r.at[zl, core], sibling, lane)
        yield
        for step in (1, -1):
            moving[step].wait_recv()
            ref = out_r.at[wrap(zl - step, Z_LO), core]
            send(ref, ref, sibling, lane)
        yield
        moving[2].wait_recv()
        send(far, far, sibling, lane)
        beside = joint(lane, out_r.at[:, 1 - core])
        yield
        beside.wait_recv()
        store = pltpu.make_async_copy(out_r, blocks[number], load_sem.at[5 + number])
        store.start()
        stores.append(store)

    interleave(*[column_part(number) for number in range(len(PARTS))])
    used = next(lanes)
    assert used == COPIES, used

    for copy in sent:
        copy.wait_send()
    for store in stores:
        store.wait()


def finish(own_grad, first, second, blocks, new_first, new_second, update):
    low_grad = own_grad[...]
    new_first[...] = beta_one * first[...] + (1.0 - beta_one) * low_grad
    new_second[...] = beta_two * second[...] + (1.0 - beta_two) * low_grad * low_grad
    cols = first.shape[1]
    for (low, width, _), part in zip(PARTS, blocks, strict=True):
        for block in range(Z_LO):
            for c in range(CORES):
                at = (block * CORES + c) * cols + low
                update[:, at : at + width] = part[block, c]


def nearest(n):
    return sorted((k for k in range(1 - n // 2, n // 2 + 1) if k), key=abs)


def on_device(Y, tokens, grad, basis, first, second):
    held, width = tokens.shape
    cols = grad.shape[1]
    rows, rank = basis.shape
    own = first.shape[0]
    deep = rank // Z_LO
    per, pair_rows = Y // Z_LO, Z_HI * own
    scratch = [
        ((held // 2, width), BF16),
        ((cols, held), BF16),
        ((Z_HI, rows, rank), BF16),
        ((Y, X, Z_HI, rows, deep), BF16),
        ((Z_LO, held, deep), BF16),
        ((Z_HI, own, cols), F32),
        ((Z_HI, own, cols), F32),
        ((own, cols), F32),
        ((rows // 2, deep), BF16),
        ((Z_LO, X, per, pair_rows, cols), F32),
        ((Z_LO, X - 1, per, pair_rows, cols), BF16),
        ((Z_LO, X - 1, per, pair_rows, cols), BF16),
        ((Z_LO, per, pair_rows, cols), F32),
        ((Y, pair_rows, cols), BF16),
        ((Y, pair_rows, cols), BF16),
        ((pair_rows, cols), BF16),
        ((pair_rows, cols), BF16),
        [
            [
                ((Y, X, pair_rows, wide), BF16),
                ((Z_HI, rows, wide), BF16),
                ((Z_LO, CORES, rows, wide), BF16),
            ]
            for _, wide, _ in PARTS
        ],
    ]

    def placed(item):
        return [placed(one) for one in item] if isinstance(item, list) else pltpu.VMEM(*item)

    placed_blocks = [jax.ShapeDtypeStruct((Z_LO, CORES, rows, wide), BF16) for _, wide, _ in PARTS]
    anywhere = pl.BlockSpec(memory_space=pl.ANY)
    own_grad, blocks = pl.pallas_call(
        functools.partial(kernel, Y),
        out_shape=(jax.ShapeDtypeStruct(first.shape, F32), placed_blocks),
        in_specs=[anywhere] * 5,
        out_specs=(anywhere, [anywhere] * len(PARTS)),
        scratch_shapes=placed(scratch)
        + [
            pltpu.SemaphoreType.DMA((COPIES,)),
            pltpu.SemaphoreType.DMA((COPIES,)),
            pltpu.SemaphoreType.DMA((6 + len(PARTS),)),
        ],
        compiler_params=pltpu.CompilerParams(
            collective_id=0, has_side_effects=True, vmem_limit_bytes=56 * 2**20
        ),
        cost_estimate=pl.CostEstimate(flops=2 * 10**9, bytes_accessed=10**7, transcendentals=0),
    )(tokens, grad.T, basis, first, second)
    high = 32
    whole = pl.BlockSpec(first.shape, lambda i: (0, 0))
    return pl.pallas_call(
        finish,
        grid=(rows // high,),
        out_shape=(
            jax.ShapeDtypeStruct(first.shape, F32),
            jax.ShapeDtypeStruct(second.shape, F32),
            jax.ShapeDtypeStruct((rows, Z_LO * CORES * cols), BF16),
        ),
        in_specs=[
            whole, whole, whole,
            [pl.BlockSpec((Z_LO, CORES, high, wide), lambda i: (0, 0, i, 0)) for _, wide, _ in PARTS],
        ],
        out_specs=(whole, whole, pl.BlockSpec((high, Z_LO * CORES * cols), lambda i: (i, 0))),
        compiler_params=pltpu.CompilerParams(vmem_limit_bytes=56 * 2**20),
        cost_estimate=pl.CostEstimate(flops=10**5, bytes_accessed=3 * 10**6, transcendentals=0),
    )(own_grad, first, second, blocks)


def solution(mesh):
    placed = (P("dp", None), P("dp", "fsdp"), P("dp", None), P("dp", "fsdp"), P("dp", "fsdp"))
    Y = mesh.shape["dp"] // (X * Z_HI)
    return jax.shard_map(
        functools.partial(on_device, Y),
        mesh=mesh,
        in_specs=placed,
        out_specs=(P("dp", "fsdp"), P("dp", "fsdp"), P("dp", None)),
        check_vma=False,
    )
```

```python
import functools
import itertools

import jax
import jax.numpy as jnp
from jax import lax
from jax.experimental import pallas as pl
from jax.experimental.pallas import tpu as pltpu
from jax.sharding import PartitionSpec as P

beta_one = 0.9
beta_two = 0.999
correct_one = 1.0 - 0.9**10
correct_two = 1.0 - 0.999**10

X = 4
Z_HI, Z_LO, CORES = 2, 4, 2
RING = Z_HI * Z_LO
PARTS = ((0, 512, "y"), (512, 512, "x"), (1024, 352, "x"))
COPIES = 67

MESH = pl.DeviceIdType.MESH
F32, BF16 = jnp.float32, jnp.bfloat16


def wrap(value, n):
    return lax.rem(value + n, n)


def interleave(*steps):
    steps = list(steps)
    while steps:
        steps = [step for step in steps if next(step, "end") != "end"]


def kernel(
    Y, tokens, grad, basis, first, second,
    own_grad, blocks,
    tok_v, grad_v, basis_v, bas, proj, first_v, second_v, grad_sum, turned,
    own, sbuf, rbuf, mid, row_s, row_r, pair_s, pair_r, part_refs,
    send_sem, recv_sem, load_sem,
):
    dp, fs = lax.axis_index("dp"), lax.axis_index("fsdp")
    zh, xy = lax.rem(dp, Z_HI), dp // Z_HI
    x, y = lax.rem(xy, X), xy // X
    core, zl = lax.rem(fs, CORES), fs // CORES
    z = zh * Z_LO + zl
    half_tokens = tok_v.shape[0]
    deep = bas.shape[4]
    rows = basis_v.shape[1]
    cols = grad.shape[0]

    def device(y_, x_, z_, core_):
        return ((y_ * X + x_) * Z_HI + z_ // Z_LO, lax.rem(z_, Z_LO) * CORES + core_)

    at_y = lambda t: device(t, x, z, core)
    at_x = lambda t: device(y, t, z, core)
    at_z = lambda t: device(y, x, t, core)
    opposite = wrap(z + Z_LO - RING, RING)
    sibling = device(y, x, z, 1 - core)
    partner = at_z(opposite)
    mirror = RING - 1 - z

    sent, lanes = [], itertools.count()

    def send(src, dst, target, lane=None):
        k = next(lanes) if lane is None else lane
        copy = pltpu.make_async_remote_copy(
            src_ref=src, dst_ref=dst, send_sem=send_sem.at[k], recv_sem=recv_sem.at[k],
            device_id=target, device_id_type=MESH,
        )
        copy.start()
        if lane is None:
            sent.append(copy)
        return copy

    def joint(lane, whole):
        copy = pltpu.make_async_remote_copy(
            src_ref=whole, dst_ref=whole, send_sem=send_sem.at[lane], recv_sem=recv_sem.at[lane],
            device_id=sibling, device_id_type=MESH,
        )
        sent.append(copy)
        return copy

    def ring_gather(n, pos, target, block, half):
        flying = [send(block(pos), block(pos), target(wrap(pos + d, n))) for d in (1, -1)]
        for s in range(1, n // 2):
            yield
            if n == X:
                yield
            lane = next(lanes) if s == n // 2 - 1 else None
            for i, d in ((0, 1), (1, -1)):
                flying[i].wait_recv()
                t = wrap(pos - d * s, n)
                if s < n // 2 - 1:
                    flying[i] = send(block(t), block(t), target(wrap(pos + d, n)))
                else:
                    send(half(t, i), half(t, i), target(wrap(pos + d, n)), lane)
        both = joint(lane, block(wrap(pos + n // 2 - n, n)))
        yield
        both.wait_recv()

    def direct_scatter(pos, target, own, sbuf, rbuf, result):
        lane = next(lanes)
        for i, k in enumerate(nearest(X)):
            t = wrap(pos + k, X)
            sbuf[i] = own[t].astype(BF16)
            send(sbuf.at[i], rbuf.at[i], target(t), lane)
        every = joint(lane, rbuf)
        yield
        total = own[pos]
        every.wait_recv()
        for i in range(X - 1):
            total = total + rbuf[i].astype(F32)
        result[...] = total

    def direct_gather(n, pos, target, block, others):
        lane = next(lanes)
        for k in nearest(n):
            send(block(pos), block(pos), target(wrap(pos + k, n)), lane)
        every = joint(lane, others)
        yield
        if n == Y:
            yield
        every.wait_recv()

    loads = [
        pltpu.make_async_copy(basis, basis_v.at[zh], load_sem.at[0]),
        pltpu.make_async_copy(first, first_v.at[zh], load_sem.at[1]),
        pltpu.make_async_copy(second, second_v.at[zh], load_sem.at[2]),
        pltpu.make_async_copy(tokens.at[pl.ds(core * half_tokens, half_tokens)], tok_v, load_sem.at[3]),
        pltpu.make_async_copy(grad, grad_v, load_sem.at[4]),
    ]
    for load in loads:
        load.start()

    barrier = pltpu.get_barrier_semaphore()
    near = [at_z(wrap(z + k - RING, RING)) for k in range(1, RING)] + [sibling]
    near += [at_x(wrap(x + k, X)) for k in nearest(X)]
    for k in nearest(Y):
        t = wrap(y + k, Y)
        near += [at_y(t), device(t, x, mirror, core)]
    for target in near:
        pl.semaphore_signal(barrier, inc=1, device_id=target, device_id_type=MESH)

    share = pl.ds(core * (rows // 2), rows // 2)
    rank, y_rows = basis_v.shape[2], basis_v.shape[2] // Y
    column = lax.broadcasted_iota(jnp.int32, (rank, deep), 1)
    row = lax.broadcasted_iota(jnp.int32, (rank, deep), 0)

    place = Z_LO * (column // y_rows) * y_rows + lax.rem(column, y_rows)

    def picks(q):
        return (row == place + q * y_rows).astype(BF16)

    own_picks, turned_picks = picks(zl), picks(Z_LO - 1 - zl)
    loads[0].wait()
    bas[y, x, zh, share] = jnp.dot(
        basis_v[zh, share], own_picks, preferred_element_type=F32
    ).astype(BF16)
    turned[...] = jnp.dot(
        basis_v[zh, share], turned_picks, preferred_element_type=F32
    ).astype(BF16)
    pl.semaphore_wait(barrier, len(near))
    ref = bas.at[y, x, zh, share]
    columns = {0: send(turned, ref, at_z(mirror))}
    for k in nearest(Y):
        t = wrap(y + k, Y)
        lane = next(lanes)
        send(ref, ref, at_y(t), lane)
        send(turned, ref, device(t, x, mirror, core), lane)
        columns[k] = joint(lane, bas.at[t, x, :, share])
    across = {}
    for k in columns:
        columns[k].wait_recv()
        ref = bas.at[wrap(y - k, Y), x, :, share]
        lane = next(lanes)
        for j in nearest(X):
            send(ref, ref, at_x(wrap(x + j, X)), lane)
        across[k] = joint(lane, bas.at[wrap(y - k, Y), pl.ds(0, X - 1), :, share])
    to_sibling = {}
    for k in across:
        across[k].wait_recv()
        ref = bas.at[wrap(y - k, Y), :, :, share]
        to_sibling[k] = send(ref, ref, sibling)

    loads[3].wait()
    inner = X * Z_HI * rows
    total = jnp.zeros((half_tokens, deep), F32)
    for k in to_sibling:
        to_sibling[k].wait_recv()
        t = wrap(y - k, Y)
        total += jnp.dot(
            tok_v[:, pl.ds(pl.multiple_of(t * inner, inner), inner)], bas[t].reshape(inner, deep),
            preferred_element_type=F32,
        )
    mine = pl.ds(core * half_tokens, half_tokens)
    proj[zl, mine] = total.astype(BF16)
    ref = proj.at[zl, mine]
    along = [next(lanes) for _ in range(1, Z_LO)]
    for k in range(1, Z_LO):
        send(ref, ref, at_z(zh * Z_LO + wrap(zl + k - Z_LO, Z_LO)), along[k - 1])
    for lane in along:
        joint(lane, ref)
    beside = [send(ref, ref, sibling)]
    loads[4].wait()
    high = own.shape[3]
    per = deep // (X * high)
    row_lane = next(lanes)

    def rank_slice(k, r):
        yield from direct_scatter(x, at_x, own.at[k], sbuf.at[k], rbuf.at[k], mid.at[r])
        for j in range(per):
            t = r + j * Z_LO
            row_s[t] = mid[r, j].astype(BF16)

            @pl.when(t != y)
            def _():
                send(row_s.at[t], row_r.at[y], at_y(t), row_lane)

    summing = []
    for k in range(Z_LO):
        r = zl
        if k:
            far = 1 + lax.rem(k - 1 + y, Z_LO - 1)
            r = wrap(zl - far, Z_LO)
            ref = proj.at[r, mine]
            pltpu.make_async_remote_copy(
                src_ref=ref, dst_ref=ref, send_sem=send_sem.at[along[0] + far - 1],
                recv_sem=recv_sem.at[along[0] + far - 1], device_id=sibling, device_id_type=MESH,
            ).wait_recv()
            beside.append(send(ref, ref, sibling))
        if k == Z_LO - 1:
            loads[1].wait()
            loads[2].wait()
            lane = next(lanes)
            for ref in (first_v.at[zh], second_v.at[zh]):
                send(ref, ref, partner, lane)
            moments = joint(lane, first_v)
        beside[k].wait_recv()
        part = lax.dot_general(
            proj[r].T, grad_v[...], (((1,), (1,)), ((), ())), preferred_element_type=F32
        ).reshape(per, X, high, cols)
        for t in range(X):
            own[k, t] = part[:, t]
        summing.append(rank_slice(k, r))
        next(summing[k])
        if k >= 2:
            next(summing[k - 2], None)
    for step in summing[Z_LO - 2 :]:
        next(step, None)
    row_sums = joint(row_lane, row_r.at[pl.ds(0, Y - 1)])

    total = mid[lax.rem(y, Z_LO), y // Z_LO]
    row_sums.wait_recv()
    for k in nearest(Y):
        total = total + row_r[wrap(y + k, Y)].astype(F32)
    pair_s[...] = total.astype(BF16)
    copy = send(pair_s, pair_r, partner)
    moments.wait_recv()
    copy.wait_recv()
    basis_pair = [send(basis_v.at[zh], basis_v.at[zh], partner)]
    low_grad = total + pair_r[...].astype(F32)
    fresh_first = beta_one * first_v[...].reshape(low_grad.shape) + (1.0 - beta_one) * low_grad
    fresh_second = (
        beta_two * second_v[...].reshape(low_grad.shape) + (1.0 - beta_two) * low_grad * low_grad
    )
    direction = (
        fresh_first / correct_one / (jnp.sqrt(fresh_second / correct_two) + 1e-08)
    ).astype(BF16)
    below = grad_sum.shape[0]
    grad_sum[...] = jnp.where(zh == 0, low_grad[:below], low_grad[below:])
    store = pltpu.make_async_copy(grad_sum, own_grad, load_sem.at[5 + len(PARTS)])
    store.start()
    stores = [store]
    for (low, width, _), refs in zip(PARTS, part_refs, strict=True):
        refs[0][y, x] = direction[:, low : low + width]

    def column_part(number):
        low, width, way = PARTS[number]
        whole, out_s, out_r = part_refs[number]
        if way == "y":
            yield from direct_gather(
                X, x, at_x, lambda t: whole.at[y, t], whole.at[y, pl.ds(0, X - 1)]
            )
            yield from ring_gather(
                Y, y, at_y, lambda t: whole.at[t],
                lambda t, h: whole.at[t, pl.ds(h * (X // 2), X // 2)],
            )
        else:
            yield from direct_gather(
                Y, y, at_y, lambda t: whole.at[t, x], whole.at[pl.ds(0, Y - 1), x]
            )
            yield from ring_gather(
                X, x, at_x, lambda t: whole.at[:, t],
                lambda t, h: whole.at[pl.ds(h * (Y // 2), Y // 2), t],
            )
        while basis_pair:
            basis_pair.pop().wait_recv()
        block = jnp.dot(
            basis_v[...].reshape(Z_HI * rows, -1), whole[...].reshape(-1, width),
            preferred_element_type=F32,
        ).astype(BF16)
        out_s[...] = block.reshape(out_s.shape)
        moving = {}
        lane = next(lanes)
        for step in (2, -2):
            to = wrap(z + step, RING)
            cut = pl.ds(0 if step > 0 else rows // 2, rows // 2)
            send(out_s.at[to // Z_LO, cut], out_r.at[zl, core, cut], at_z(to), lane)
        for step in (1, -1):
            to = wrap(z + step, RING)
            moving[step] = send(out_s.at[to // Z_LO], out_r.at[zl, core], at_z(to))
        far = out_r.at[wrap(zl + 2 - Z_LO, Z_LO), core]
        moving[2] = joint(lane, far)
        out_r[zl, core] = out_s[zh]
        lane = next(lanes)
        send(out_r.at[zl, core], out_r.at[zl, core], sibling, lane)
        yield
        for step in (1, -1):
            moving[step].wait_recv()
            ref = out_r.at[wrap(zl - step, Z_LO), core]
            send(ref, ref, sibling, lane)
        yield
        moving[2].wait_recv()
        send(far, far, sibling, lane)
        beside = joint(lane, out_r.at[:, 1 - core])
        yield
        beside.wait_recv()
        store = pltpu.make_async_copy(out_r, blocks[number], load_sem.at[5 + number])
        store.start()
        stores.append(store)

    interleave(*[column_part(number) for number in range(len(PARTS))])
    used = next(lanes)
    assert used == COPIES, used

    for copy in sent:
        copy.wait_send()
    for store in stores:
        store.wait()


def finish(own_grad, first, second, blocks, new_first, new_second, update):
    low_grad = own_grad[...]
    new_first[...] = beta_one * first[...] + (1.0 - beta_one) * low_grad
    new_second[...] = beta_two * second[...] + (1.0 - beta_two) * low_grad * low_grad
    cols = first.shape[1]
    for (low, width, _), part in zip(PARTS, blocks, strict=True):
        for block in range(Z_LO):
            for c in range(CORES):
                at = (block * CORES + c) * cols + low
                update[:, at : at + width] = part[block, c]


def nearest(n):
    return sorted((k for k in range(1 - n // 2, n // 2 + 1) if k), key=abs)


def on_device(Y, tokens, grad, basis, first, second):
    held, width = tokens.shape
    cols = grad.shape[1]
    rows, rank = basis.shape
    own = first.shape[0]
    deep = rank // Z_LO
    per, pair_rows = Y // Z_LO, Z_HI * own
    scratch = [
        ((held // 2, width), BF16),
        ((cols, held), BF16),
        ((Z_HI, rows, rank), BF16),
        ((Y, X, Z_HI, rows, deep), BF16),
        ((Z_LO, held, deep), BF16),
        ((Z_HI, own, cols), F32),
        ((Z_HI, own, cols), F32),
        ((own, cols), F32),
        ((rows // 2, deep), BF16),
        ((Z_LO, X, per, pair_rows, cols), F32),
        ((Z_LO, X - 1, per, pair_rows, cols), BF16),
        ((Z_LO, X - 1, per, pair_rows, cols), BF16),
        ((Z_LO, per, pair_rows, cols), F32),
        ((Y, pair_rows, cols), BF16),
        ((Y, pair_rows, cols), BF16),
        ((pair_rows, cols), BF16),
        ((pair_rows, cols), BF16),
        [
            [
                ((Y, X, pair_rows, wide), BF16),
                ((Z_HI, rows, wide), BF16),
                ((Z_LO, CORES, rows, wide), BF16),
            ]
            for _, wide, _ in PARTS
        ],
    ]

    def placed(item):
        return [placed(one) for one in item] if isinstance(item, list) else pltpu.VMEM(*item)

    placed_blocks = [jax.ShapeDtypeStruct((Z_LO, CORES, rows, wide), BF16) for _, wide, _ in PARTS]
    anywhere = pl.BlockSpec(memory_space=pl.ANY)
    own_grad, blocks = pl.pallas_call(
        functools.partial(kernel, Y),
        out_shape=(jax.ShapeDtypeStruct(first.shape, F32), placed_blocks),
        in_specs=[anywhere] * 5,
        out_specs=(anywhere, [anywhere] * len(PARTS)),
        scratch_shapes=placed(scratch)
        + [
            pltpu.SemaphoreType.DMA((COPIES,)),
            pltpu.SemaphoreType.DMA((COPIES,)),
            pltpu.SemaphoreType.DMA((6 + len(PARTS),)),
        ],
        compiler_params=pltpu.CompilerParams(
            collective_id=0, has_side_effects=True, vmem_limit_bytes=56 * 2**20
        ),
        cost_estimate=pl.CostEstimate(flops=2 * 10**9, bytes_accessed=10**7, transcendentals=0),
    )(tokens, grad.T, basis, first, second)
    high = 32
    whole = pl.BlockSpec(first.shape, lambda i: (0, 0))
    return pl.pallas_call(
        finish,
        grid=(rows // high,),
        out_shape=(
            jax.ShapeDtypeStruct(first.shape, F32),
            jax.ShapeDtypeStruct(second.shape, F32),
            jax.ShapeDtypeStruct((rows, Z_LO * CORES * cols), BF16),
        ),
        in_specs=[
            whole, whole, whole,
            [pl.BlockSpec((Z_LO, CORES, high, wide), lambda i: (0, 0, i, 0)) for _, wide, _ in PARTS],
        ],
        out_specs=(whole, whole, pl.BlockSpec((high, Z_LO * CORES * cols), lambda i: (i, 0))),
        compiler_params=pltpu.CompilerParams(vmem_limit_bytes=56 * 2**20),
        cost_estimate=pl.CostEstimate(flops=10**5, bytes_accessed=3 * 10**6, transcendentals=0),
    )(own_grad, first, second, blocks)


def solution(mesh):
    placed = (P("dp", None), P("dp", "fsdp"), P("dp", None), P("dp", "fsdp"), P("dp", "fsdp"))
    Y = mesh.shape["dp"] // (X * Z_HI)
    return jax.shard_map(
        functools.partial(on_device, Y),
        mesh=mesh,
        in_specs=placed,
        out_specs=(P("dp", "fsdp"), P("dp", "fsdp"), P("dp", None)),
        check_vma=False,
    )
```
